32 devices in a mesh: groups: 2 (over x), block: 16 (over z, y, core).
Axes of the slice: x: 2, y: 2, z: 4, core: 2. Of those that a mesh axis runs over, the one named last changes fastest.
Arguments:
- slices: bfloat16 [4, 12288, 2048], P(None, ('groups', 'block')), parts along dimension 1, may hold values from -0.75 to 0.75
- slice_mix: float32 [4, 4], replicated, may hold values from -1 to 1
- lengths: int32 [32, 4], P(('groups', 'block')), parts along dimension 0, may hold values from 1 to 96, 288 in all within a row
- search_step: bfloat16 [4096], P('groups'), parts along dimension 0, may hold values from -0.125 to 0.125
Outputs:
- schur_matrix: float32 [4096, 2048], P(('groups', 'block')), parts along dimension 0
- schur_step: float32 [4096], P('groups'), parts along dimension 0
The draws below stay inside these ranges and needn't reach their ends.
There are 2 independent parts, one for each index of `groups`. The reference program is written for one: setup_inputs(seed, part) draws one part's arguments, and reference() takes and returns one part's arrays. A program takes and returns all parts, laid end to end along the dimension named above; an argument that names none is the same for every part. Nothing has to cross between parts.
Inputs may be any that keep to these rules, and one draw needn't show every extreme that they name: `lengths`: each row holds the used rows of one device's 4 blocks; a row sums to 288 and its largest entry is 96.
All inputs are finite; a program needn't handle non-finite values.
Results may differ from the reference program's by a relative error of at most 0.0055.
Values sent between devices are 32-bit elements; how exact they have to be, the bound alone decides.
No kernel may reach another device: no remote copies, remote signals or barrier semaphores. Data moves between devices by JAX's collectives and lax.ppermute only.
A program may use at most 128 MiB of HBM per device.

```python
import math
import jax
import jax.numpy as jnp
import numpy as np
from jax import lax

V = 2048
SLICES = 4
BLK_DEV = 4
BROWS = 96
ROWS_DEV = 384
SHARDS = 16
ROWS = 6144
N_BLOCK = 16


def spiked(array, stream_key, source, target, shards_of, factor):
    owner, partner = [(jnp.arange(array.shape[axis_at]) // (array.shape[axis_at] // shards_of)).reshape([-1 if axis == axis_at else 1 for axis in range(array.ndim)]) for axis_at in (source, target)]
    chosen = jax.random.permutation(stream_key, shards_of)[partner]
    strong = (owner == chosen) | (owner == (partner + shards_of // 2) % shards_of)
    return jnp.where(strong, factor * array, array)


def steps_of(key, shape, split, smallest, largest):
    def one(axis_at, shards_of):
        steps = jax.random.uniform(jax.random.fold_in(jax.random.fold_in(key, 6), axis_at), (shards_of,), jnp.float32, smallest / len(split), largest / len(split))
        return jnp.repeat(jnp.exp(steps), shape[axis_at] // shards_of).reshape((-1,) + (1,) * (len(shape) - axis_at - 1))

    level = one(*split[0])
    for cut in split[1:]:
        level = level * one(*cut)
    return level


def length_profile(amount, total, limit, skew):
    portions = [(1 << 20) // math.isqrt(standing ** skew) + 1 for standing in range(2, amount + 1)]
    rest, holding = total - limit - (amount - 1), [1] * (amount - 1)
    while rest > 0:
        movable = [i for i in range(amount - 1) if holding[i] < limit]
        pool, remaining = sum([portions[i] for i in movable]), rest
        for i in movable:
            more = min(limit - holding[i], max(1, remaining * portions[i] // pool), rest)
            holding[i] = holding[i] + more
            rest = rest - more
    return np.array([limit] + holding)


def ragged_sizes(key, count, total, limit, lean):
    if count == 2:
        one = jax.random.randint(key, (), max(1, total - limit), min(limit, total - 1) + 1)
        return jnp.stack([one, total - one])
    sizes = jnp.asarray(length_profile(count, total, limit, lean), jnp.int32)
    couples = (count - 1) // 2
    donor, receiver = sizes[1:1 + 2 * couples:2], sizes[2:2 + 2 * couples:2]
    slack = jnp.minimum(donor - 1, limit - receiver)
    shifted = jax.random.randint(jax.random.fold_in(key, 1), (couples,), 0, 1 << 20) % (slack + 1)
    sizes = sizes.at[1:1 + 2 * couples:2].set(donor - shifted).at[2:2 + 2 * couples:2].set(receiver + shifted)
    return sizes[jax.random.permutation(jax.random.fold_in(key, 2), count)]


def centred(stream_key, dims, scale, limit, shards=(), kind=jnp.bfloat16):
    array = jax.random.normal(stream_key, dims, jnp.float32) * scale
    if len(shards) > 0:
        array = steps_of(stream_key, dims, shards, -0.22, 0.18) * array
    return jnp.clip(array, min=-limit, max=limit).astype(kind)


def noise_with(own_key, shape, scale, most, shards, heavy, held_as=jnp.bfloat16):
    drawn = scale * jax.random.normal(own_key, shape, jnp.float32)
    if shards:
        drawn = drawn * steps_of(own_key, shape, shards, -0.22, 0.18)
    return jnp.clip(spiked(drawn, jax.random.fold_in(own_key, 3), *heavy), -most, most).astype(held_as)


def setup_inputs(seed: int = 0, part: int = 0) -> dict:
    key_of = jax.random.split(jax.random.key(seed), 5)
    own_keys = jax.random.split(jax.random.fold_in(key_of[4], part), 5)
    slices = noise_with(own_keys[0], (SLICES, ROWS, V), (0.7 * (3 * BROWS * N_BLOCK) ** -0.25), 0.75, ((1, 16),), (1, 2, 16, 2.0))
    slice_mix = jnp.clip(jax.random.uniform(key_of[1], (SLICES, SLICES), jnp.float32, -1.0, 1.0), -1.0, 1.0)
    lengths = jax.vmap(lambda own: ragged_sizes(own, BLK_DEV, 3 * BROWS, BROWS, 1))(jax.random.split(own_keys[2], SHARDS)).reshape((SHARDS, BLK_DEV)).astype(jnp.int32)
    search_step = centred(own_keys[3], (V,), (V ** -0.5), 0.125)
    return dict(slices=slices, slice_mix=slice_mix, lengths=lengths, search_step=search_step)


def coupling_of(slice_mix):
    symmetric = (slice_mix + slice_mix.T) * 0.5
    return symmetric * (1.0 - jnp.eye(SLICES, dtype=jnp.float32))


def mix_slices(shard_slices, coupling, row_used):
    rows_out = []
    for target in range(SLICES):
        total = coupling[target, 0] * shard_slices[0].astype(jnp.float32)
        for source in range(1, SLICES):
            total = total + coupling[target, source] * shard_slices[source].astype(jnp.float32)
        rows_out.append(total)
    stacked = jnp.stack(rows_out) * row_used[None, :, None]
    return stacked.astype(jnp.bfloat16)


def reference(slices, slice_mix, lengths, search_step):
    coupling = coupling_of(slice_mix)
    position = lax.broadcasted_iota(jnp.int32, (BLK_DEV, BROWS), 1)

    def accumulate(total, shard):
        shard_slices = lax.dynamic_slice_in_dim(slices, (shard * ROWS_DEV).astype(jnp.int32), ROWS_DEV, 1)
        shard_lengths = lax.dynamic_slice_in_dim(lengths, shard.astype(jnp.int32), 1, 0)[0]
        row_used = (position < shard_lengths[:, None]).reshape(-1).astype(jnp.float32)
        mixed = mix_slices(shard_slices, coupling, row_used)
        left = shard_slices.reshape(SLICES * ROWS_DEV, V)
        right = mixed.reshape(SLICES * ROWS_DEV, V)
        term = lax.dot_general(left, right, (((0,), (0,)), ((), ())), preferred_element_type=jnp.float32)
        return total + term, None

    schur_matrix, _ = lax.scan(accumulate, jnp.zeros((V, V), jnp.float32), jnp.arange(SHARDS, dtype=jnp.int32))
    schur_step = jnp.dot(schur_matrix, search_step.astype(jnp.float32), precision=lax.Precision.HIGHEST)
    return schur_matrix, schur_step
```

```python
import functools

import jax
import jax.numpy as jnp
from jax import lax
from jax.experimental import pallas as pl
from jax.experimental.pallas import tpu as pltpu
from jax.sharding import PartitionSpec as P

AXIS = "block"
CORES = 2
COLS = 2
DIMS0 = (((0,), (0,)), ((), ()))
DIMS1 = (((1,), (1,)), ((), ()))
VMEM = pl.BlockSpec(memory_space=pltpu.VMEM)
SMEM = pl.BlockSpec(memory_space=pltpu.SMEM)


def row_mask(lengths_ref, rows, width):
    blocks = lengths_ref.shape[1]
    step = rows // blocks
    row = lax.broadcasted_iota(jnp.int32, (rows, width), 0)
    limit = jnp.zeros((rows, width), jnp.int32)
    for j in range(blocks):
        limit = jnp.where(row >= j * step, j * step + lengths_ref[0, j], limit)
    return row < limit


def mix_kernel(mix_ref, lengths_ref, slices_ref, left_ref, right_ref):
    count, rows, width = slices_ref.shape
    used = row_mask(lengths_ref, rows, width)
    s = [slices_ref[k] for k in range(count)]
    f = [a.astype(jnp.float32) for a in s]
    for k in range(count):
        total = None
        for l in range(count):
            if l != k:
                term = ((mix_ref[k, l] + mix_ref[l, k]) * 0.5) * f[l]
                total = term if total is None else total + term
        right_ref[k * rows : (k + 1) * rows, :] = jnp.where(used, total, 0.0).astype(jnp.bfloat16)
        left_ref[:, k * rows : (k + 1) * rows] = s[k].T


def mix(slices, slice_mix, lengths, tile):
    count, rows, width = slices.shape
    depth = count * rows
    return pl.pallas_call(
        mix_kernel,
        grid=(width // tile,),
        in_specs=[SMEM, SMEM, pl.BlockSpec((count, rows, tile), lambda i: (0, 0, i))],
        out_specs=[
            pl.BlockSpec((tile, depth), lambda i: (i, 0)),
            pl.BlockSpec((depth, tile), lambda i: (0, i)),
        ],
        out_shape=[
            jax.ShapeDtypeStruct((width, depth), jnp.bfloat16),
            jax.ShapeDtypeStruct((depth, width), jnp.bfloat16),
        ],
        compiler_params=pltpu.CompilerParams(vmem_limit_bytes=24 << 20),
        name="mix",
    )(slice_mix, lengths, slices)


def place():
    me = lax.axis_index(AXIS)
    core = lax.rem(me, CORES)
    y = lax.rem(me // CORES, COLS)
    z = me // (CORES * COLS)
    return z, y, core


def tiles_kernel(lines, unit, jobs, left_ref, right_ref, *refs):
    outs, acc = refs[:-1], refs[-1]
    chips = lines * COLS
    z, y, core = place()
    for n, (shift, sy) in enumerate(jobs):
        own_ref, other_ref = outs[2 * n], outs[2 * n + 1]
        half = 2 * shift == chips

        def step(sz, carry):
            row = lax.rem(z + sz, lines) * COLS + (y ^ sy)
            col = lax.rem(row + shift, chips)
            acc[...] = jnp.dot(
                left_ref[pl.ds(pl.multiple_of(row * 2 * unit, 2 * unit), 2 * unit), :],
                right_ref[:, pl.ds(pl.multiple_of(col * 2 * unit, 2 * unit), 2 * unit)],
                preferred_element_type=jnp.float32,
            )
            flip = (row >= shift).astype(jnp.int32) if half else 0
            for ref, owner in ((own_ref, core), (other_ref, 1 - core)):
                for j in range(ref.shape[1]):
                    first = pl.multiple_of((owner ^ j ^ flip) * unit, unit)
                    ref[sz, j] = acc[pl.ds(pl.multiple_of(owner * unit, unit), unit), pl.ds(first, unit)]
            return carry

        lax.fori_loop(0, lines, step, 0)


def tiles(left, right, jobs, lines, unit):
    shapes = []
    for shift, _ in jobs:
        blocks = 1 if 2 * shift == lines * COLS else CORES
        shapes += [jax.ShapeDtypeStruct((lines, blocks, unit, unit), jnp.float32)] * 2
    flops = 2 * len(jobs) * lines * (2 * unit) ** 2 * left.shape[1]
    out = pl.pallas_call(
        functools.partial(tiles_kernel, lines, unit, jobs),
        in_specs=[VMEM, VMEM],
        out_specs=[VMEM] * len(shapes),
        out_shape=shapes,
        scratch_shapes=[pltpu.VMEM((2 * unit, 2 * unit), jnp.float32)],
        cost_estimate=pl.CostEstimate(flops=flops, bytes_accessed=0, transcendentals=0),
        compiler_params=pltpu.CompilerParams(vmem_limit_bytes=24 << 20),
        name="tiles",
    )(left, right)
    return [(out[2 * n], out[2 * n + 1]) for n in range(len(jobs))]


def vector_kernel(left_ref, right_ref, step_ref, out_ref):
    x = jnp.broadcast_to(step_ref[...], (8, step_ref.shape[1]))
    applied = lax.dot_general(x, right_ref[...], DIMS1, preferred_element_type=jnp.float32)
    head = applied.astype(jnp.bfloat16)
    tail = (applied - head.astype(jnp.float32)).astype(jnp.bfloat16)
    row = lax.broadcasted_iota(jnp.int32, applied.shape, 0)
    both = jnp.where(row == 0, head.astype(jnp.float32), jnp.where(row == 1, tail.astype(jnp.float32), 0.0))
    share = lax.dot_general(both.astype(jnp.bfloat16), left_ref[...], DIMS1, preferred_element_type=jnp.float32)
    out_ref[...] = share[0:1, :] + share[1:2, :]


def vector(left, right, step):
    return pl.pallas_call(
        vector_kernel,
        in_specs=[VMEM] * 3,
        out_specs=VMEM,
        out_shape=jax.ShapeDtypeStruct((1, step.shape[0]), jnp.float32),
        compiler_params=pltpu.CompilerParams(vmem_limit_bytes=24 << 20),
        name="vector",
    )(left, right, step.reshape(1, -1))


def join_kernel(lines, unit, plan, *refs):
    chips = lines * COLS
    out_ref = refs[-1]
    z, y, core = place()
    chip = z * COLS + y
    for ref, index, shift, sign, j, mirrored in plan:
        col = lax.rem(chip + sign * shift + chips, chips)
        if 2 * shift == chips:
            low = (chip >= shift).astype(jnp.int32)
            other = core ^ (1 - low) if mirrored else core ^ low
        else:
            other = core ^ j
        value = refs[ref][...] if index is None else refs[ref][index]
        out_ref[:, pl.ds(pl.multiple_of((col * CORES + other) * unit, unit), unit)] = value.T if mirrored else value


def join(arrays, plan, lines, unit, width):
    return pl.pallas_call(
        functools.partial(join_kernel, lines, unit, plan),
        in_specs=[VMEM] * len(arrays),
        out_specs=VMEM,
        out_shape=jax.ShapeDtypeStruct((unit, width), jnp.float32),
        compiler_params=pltpu.CompilerParams(vmem_limit_bytes=24 << 20),
        name="join",
    )(*arrays)


def flat(z, y, core):
    return (z * COLS + y) * CORES + core


def send(x, lines, to):
    pairs = []
    for z in range(lines):
        for y in range(COLS):
            for core in range(CORES):
                target = to(z, y, core)
                if target is not None:
                    pairs.append((flat(z, y, core), flat(*target)))
    return lax.ppermute(x, AXIS, pairs)


def to_core(z, y, core):
    return z, y, 1 - core


def to_col(z, y, core):
    return z, 1 - y, core


def along_line(parts, lines):
    parts = list(parts)
    for r in range(1, lines):
        up = send(parts[lines - r], lines, lambda z, y, c: (z + 1, y, c) if z < r else None)
        down = send(parts[r], lines, lambda z, y, c: (z - 1, y, c) if z >= lines - r else None)
        to_up, to_down = lines - r - 1, (r + 1) % lines
        if to_up == to_down:
            parts[to_up] = parts[to_up] + up + down
        else:
            parts[to_up] = parts[to_up] + up
            parts[to_down] = parts[to_down] + down
    return parts[0]


def mirrored(block, lines, shift, j):
    chips = lines * COLS

    def to(z, y, core):
        chip = z * COLS + y
        flip = int(chip >= shift) if 2 * shift == chips else j
        other = (chip + shift) % chips
        return other // COLS, other % COLS, core ^ flip

    return send(block, lines, to)


def total_of(share, lines):
    share = share + send(share, lines, to_core)
    share = share + send(share, lines, to_col)
    hop = 1
    while hop < lines:
        share = share + send(share, lines, lambda z, y, c: (z ^ hop, y, c))
        hop *= 2
    return share


def halved(slices, slice_mix, lengths, search_step, lines, unit):
    width = slices.shape[2]
    chips = lines * COLS
    left, right = mix(slices, slice_mix, lengths, 2 * unit)
    order = [2, 4, 1, 3, 0]
    parts = {}
    jobs = [(order[0], 1)]
    parts[jobs[0]] = tiles(left, right, jobs, lines, unit)[0]
    jobs = [(k, sy) for k in order for sy in (1, 0)][1:]
    for job, out in zip(jobs, tiles(left, right, jobs, lines, unit)):
        parts[job] = out
    step = total_of(vector(left, right, search_step), lines)
    arrays, plan = [], []
    for k in order:
        q = {}
        for sy in (1, 0):
            own, other = parts[k, sy]
            q[sy] = own + send(other, lines, to_core)
        if k == 4:
            both = [jnp.concatenate([q[1][s : s + 1], q[0][s : s + 1]]) for s in range(lines)]
            done = along_line(both, lines)
            done = done[1] + send(done[0], lines, to_col)
        else:
            came = send(q[1], lines, to_col)
            done = along_line([q[0][s] + came[s] for s in range(lines)], lines)
        for j in range(done.shape[0]):
            plan.append((len(arrays), j, k, 1, j, False))
        arrays.append(done)
        if k:
            for j in range(done.shape[0]):
                plan.append((len(arrays), None, k, -1, j, True))
                arrays.append(mirrored(done[j], lines, k, j))
    return join(arrays, plan, lines, unit, width), step.reshape(-1)


def coupled(slices, slice_mix, lengths):
    count = slices.shape[0]
    coupling = (slice_mix + slice_mix.T) * 0.5 * (1.0 - jnp.eye(count, dtype=jnp.float32))
    blocks = lengths.shape[1]
    position = lax.broadcasted_iota(jnp.int32, (blocks, slices.shape[1] // blocks), 1)
    used = (position < lengths[0][:, None]).reshape(-1).astype(jnp.float32)
    out = []
    for k in range(count):
        total = coupling[k, 0] * slices[0].astype(jnp.float32)
        for l in range(1, count):
            total = total + coupling[k, l] * slices[l].astype(jnp.float32)
        out.append(total)
    return (jnp.stack(out) * used[None, :, None]).astype(jnp.bfloat16)


def whole(slices, slice_mix, lengths, search_step):
    width = slices.shape[2]
    left = slices.reshape(-1, width)
    right = coupled(slices, slice_mix, lengths).reshape(-1, width)
    rows = lax.psum_scatter(
        lax.dot_general(left, right, DIMS0, preferred_element_type=jnp.float32), AXIS, scatter_dimension=0, tiled=True
    )
    applied = jnp.dot(right, search_step, preferred_element_type=jnp.float32)
    head = applied.astype(jnp.bfloat16)
    tail = (applied - head.astype(jnp.float32)).astype(jnp.bfloat16)
    share = lax.dot_general(left, head, DIMS0, preferred_element_type=jnp.float32)
    share = share + lax.dot_general(left, tail, DIMS0, preferred_element_type=jnp.float32)
    return rows, lax.psum(share, AXIS)


def solution(mesh):
    devices = mesh.shape[AXIS]

    def on_device(slices, slice_mix, lengths, search_step):
        unit = slices.shape[2] // devices
        if devices == 16 and unit % 128 == 0:
            return halved(slices, slice_mix, lengths, search_step, devices // (COLS * CORES), unit)
        return whole(slices, slice_mix, lengths, search_step)

    return jax.shard_map(
        on_device,
        mesh=mesh,
        in_specs=(
            P(None, ("groups", AXIS), None),
            P(),
            P(("groups", AXIS), None),
            P("groups"),
        ),
        out_specs=(P(("groups", AXIS), None), P("groups")),
        check_vma=False,
    )
```

```python
import functools

import jax
import jax.numpy as jnp
from jax import lax
from jax.experimental import pallas as pl
from jax.experimental.pallas import tpu as pltpu
from jax.sharding import PartitionSpec as P

AXIS = "block"
CORES = 2
TILE = 16
LANES = 128
DIMS0 = (((0,), (0,)), ((), ()))
DIMS1 = (((1,), (1,)), ((), ()))
VMEM = pl.BlockSpec(memory_space=pltpu.VMEM)
HBM = pl.BlockSpec(memory_space=pltpu.HBM)
ANY = pl.BlockSpec(memory_space=pl.ANY)

PIECES = {
    "a": ((1, 2), (1, 2, 4)),
    "b": ((3, 4), (2, 1, 4)),
    "c": ((0,), (1, 2, 4)),
}
FIRST, CARRIER = "a", "b"
ORDER = "Ka Kb a1 Kc b1 c1 a2 b2 a3 b3 c2 a4 c3 b4"


class Sizes:
    def __init__(self, devices, slices, lengths):
        self.devices = devices
        self.chips = devices // CORES
        self.count, self.rows, self.width = slices.shape
        self.blocks = lengths.shape[1]
        self.unit = self.width // devices
        self.step = self.rows // self.blocks
        most = self.step // TILE + ((self.blocks - 2) * self.step + (self.blocks - 1) * (TILE - 1)) // TILE
        self.chunk = 256 // self.count
        self.chunks = -(-most * TILE // self.chunk)
        self.tiles = self.chunks * self.chunk // TILE
        self.depth = self.count * self.chunks * self.chunk
        self.extended = self.width + 2 * CORES * self.unit

    def parts(self, shift):
        return 1 if 2 * shift == self.chips else CORES

    def piece_blocks(self, shifts):
        return sum(self.parts(k) for k in shifts)


def fits(devices, slices, lengths):
    unit, step = slices.shape[2] // devices, slices.shape[1] // lengths.shape[1]
    return devices == 16 and unit == LANES and slices.shape[0] == 4 and step % TILE == 0


def place():
    me = lax.axis_index(AXIS)
    return me // CORES, lax.rem(me, CORES)


def load_and_mix(sz, mix_hbm, lengths_hbm, slices_hbm, left_ref, right_ref, raw, mix_ref, lengths_ref, table, sems):
    first = pltpu.make_async_copy(lengths_hbm, lengths_ref, sems.at[sz.chunks])
    second = pltpu.make_async_copy(mix_hbm, mix_ref, sems.at[sz.chunks + 1])
    first.start()
    second.start()
    first.wait()
    for p in range(sz.tiles + 1):
        table[0, p] = 0
        table[1, p] = 0
    at = jnp.int32(0)
    for j in range(sz.blocks):
        for i in range(sz.step // TILE):
            inside = lengths_ref[0, j] - i * TILE
            at_safe = jnp.minimum(at, sz.tiles)
            table[0, at_safe] = jnp.where(inside > 0, j * sz.step + i * TILE, 0)
            table[1, at_safe] = jnp.clip(inside, 0, TILE)
            at = at + (inside > 0).astype(jnp.int32)
    per = sz.chunk // TILE
    for p in range(sz.tiles):
        source = pl.multiple_of(table[0, p], TILE)
        pltpu.make_async_copy(
            slices_hbm.at[:, pl.ds(source, TILE), :], raw.at[:, pl.ds(p * TILE, TILE), :], sems.at[p // per]
        ).start()
    second.wait()
    weight = {}
    for k in range(sz.count):
        for l in range(sz.count):
            if l != k:
                weight[k, l] = (mix_ref[k, l] + mix_ref[l, k]) * 0.5
    span = 4 * LANES
    wide = 2 * LANES

    def one_chunk(g, carry):
        here = pl.ds(pl.multiple_of(g * sz.chunk, sz.chunk), sz.chunk)
        pltpu.make_async_copy(slices_hbm.at[:, pl.ds(0, sz.chunk), :], raw.at[:, here, :], sems.at[g]).wait()
        base = g * sz.count * sz.chunk
        for p in range(per):
            row = lax.broadcasted_iota(jnp.int32, (TILE, LANES), 0)
            used = jnp.tile(row < table[1, g * per + p], (1, span // LANES))

            def columns(i, carry):
                cols = pl.ds(pl.multiple_of(i * span, span), span)
                rows = pl.ds(pl.multiple_of(g * sz.chunk + p * TILE, TILE), TILE)
                f = [raw[k, rows, cols].astype(jnp.float32) for k in range(sz.count)]
                for k in range(sz.count):
                    total = None
                    for l in range(sz.count):
                        if l != k:
                            term = weight[k, l] * f[l]
                            total = term if total is None else total + term
                    value = jnp.where(used, total, 0.0).astype(jnp.bfloat16)
                    to = pl.ds(pl.multiple_of(base + k * sz.chunk + p * TILE, TILE), TILE)
                    right_ref[to, cols] = value
                return carry

            lax.fori_loop(0, sz.width // span, columns, 0, unroll=2)

        def turn(i, carry):
            cols = pl.ds(pl.multiple_of(i * wide, wide), wide)
            block = raw[:, here, cols].reshape(sz.count * sz.chunk, wide)
            left_ref[cols, pl.ds(pl.multiple_of(base, LANES), sz.count * sz.chunk)] = block.T
            return carry

        lax.fori_loop(0, sz.width // wide, turn, 0, unroll=2)
        rows = pl.ds(pl.multiple_of(base, LANES), sz.count * sz.chunk)
        right_ref[rows, sz.width :] = right_ref[rows, : sz.extended - sz.width]
        return carry

    lax.fori_loop(0, sz.chunks, one_chunk, 0)


def runs(shifts):
    out = []
    for k in shifts:
        if out and out[-1][-1] + 1 == k:
            out[-1].append(k)
        else:
            out.append([k])
    return out


def multiply(sz, piece, left_ref, right_ref, outs, acc):
    shifts, order = piece
    unit, chips = sz.unit, sz.chips
    blocks = sz.piece_blocks(shifts)
    wide = CORES * unit
    chip, core = place()
    half = chips // 2
    for bit in (1, 0):
        other_ref, own_ref = outs[2 * (1 - bit)], outs[2 * (1 - bit) + 1]

        def one(index, carry):
            slot = bit * order[0]
            for n, mask in enumerate(order[1:]):
                slot = slot + mask * ((index >> (len(order) - 2 - n)) & 1)
            row = chip ^ slot
            lhs = left_ref[pl.ds(pl.multiple_of(row * wide, wide), wide), :]
            at = 0
            for run in runs(shifts):
                col = lax.rem(row + run[0], chips)
                size = wide * len(run)
                acc[:, :size] = jnp.dot(
                    lhs, right_ref[:, pl.ds(pl.multiple_of(col * wide, wide), size)], preferred_element_type=jnp.float32
                )
                for n, k in enumerate(run):
                    for h in range(sz.parts(k)):
                        for ref, owner in ((other_ref, 1 - core), (own_ref, core)):
                            if 2 * k == chips:
                                rows, cols = owner, owner ^ (row >= half).astype(jnp.int32)
                            else:
                                rows, cols = owner ^ h, owner
                            ref[pl.ds(pl.multiple_of((index * blocks + at + h) * unit, unit), unit), :] = acc[
                                pl.ds(pl.multiple_of(rows * unit, unit), unit),
                                pl.ds(pl.multiple_of(n * wide + cols * unit, unit), unit),
                            ]
                    at += sz.parts(k)
            return carry

        lax.fori_loop(0, chips // 2, one, 0)


def vector(sz, left_ref, right_ref, step_ref, outs):
    x = jnp.broadcast_to(step_ref[...], (8, sz.width))
    applied = lax.dot_general(x, right_ref[:, : sz.width], DIMS1, preferred_element_type=jnp.float32)
    head = applied.astype(jnp.bfloat16).astype(jnp.float32)
    row = lax.broadcasted_iota(jnp.int32, applied.shape, 0)
    both = jnp.where(row == 0, head, jnp.where(row == 1, applied - head, 0.0)).astype(jnp.bfloat16)
    share = lax.dot_general(both, left_ref[...], DIMS1, preferred_element_type=jnp.float32)
    share = share[0:1, :] + share[1:2, :]
    extra = sz.width // LANES
    for ref in outs:
        first = ref.shape[0] - extra
        for r in range(extra):
            ref[first + r : first + r + 1, :] = share[:, r * LANES : (r + 1) * LANES]


def add_rows(to, at, size, *terms):
    block = LANES if size % LANES == 0 else size

    def one(i, carry):
        total = None
        for ref, first in terms:
            value = ref[pl.ds(pl.multiple_of(first + i * block, 8), block), :]
            total = value if total is None else total + value
        to[pl.ds(pl.multiple_of(at + i * block, 8), block), :] = total
        return carry

    lax.fori_loop(0, size // block, one, 0)


class Chain:
    def __init__(self):
        self.token = None

    def call(self, name, body, inputs, shapes, scratch=(), specs=None, flops=0, vmem=24):
        specs = list(specs or [VMEM] * len(inputs))
        inputs = list(inputs)
        count = len(inputs)
        if self.token is not None:
            inputs.append(self.token)
            specs.append(ANY)

        def kernel(*refs):
            body(*refs[:count], *refs[len(inputs) :])

        out = pl.pallas_call(
            kernel,
            in_specs=specs,
            out_specs=[VMEM] * len(shapes),
            out_shape=[jax.ShapeDtypeStruct(s, d) for s, d in shapes],
            scratch_shapes=list(scratch),
            cost_estimate=pl.CostEstimate(flops=flops, bytes_accessed=0, transcendentals=0),
            compiler_params=pltpu.CompilerParams(vmem_limit_bytes=vmem << 20),
            name=name,
        )(*inputs)
        self.token = out[-1]
        return out


def send(x, chips, to):
    pairs = []
    for chip in range(chips):
        for core in range(CORES):
            other, its_core = to(chip, core)
            pairs.append((chip * CORES + core, other * CORES + its_core))
    return lax.ppermute(x, AXIS, pairs)


def to_core(x, chips):
    return send(x, chips, lambda m, c: (m, 1 - c))


def across(x, chips, mask):
    return send(x, chips, lambda m, c: (m ^ mask, c))


def mirror(x, chips, shift):
    def to(m, c):
        flip = int(m >= shift) if 2 * shift == chips else 0
        return (m + shift) % chips, c ^ flip

    return send(x, chips, to)


def halved(sz, slices, slice_mix, lengths, search_step):
    chips, unit, f32 = sz.chips, sz.unit, jnp.float32
    chain = Chain()
    extra = sz.width // LANES
    state = {}
    step_row = search_step.reshape(1, -1)

    def tail(name):
        return extra if name == CARRIER else 0

    def start(name):
        piece = PIECES[name]
        shifts, order = piece
        rows = chips // 2 * sz.piece_blocks(shifts) * unit
        shapes = [((rows + tail(name), LANES), f32)] * 2 + [((rows, LANES), f32)] * 2
        wide = CORES * unit
        acc = pltpu.VMEM((wide, wide * max(len(r) for r in runs(shifts))), f32)
        flops = 2 * chips * wide * wide * len(shifts) * sz.depth
        if name == FIRST:

            def body(mix_hbm, lengths_hbm, slices_hbm, *refs):
                left_ref, right_ref = refs[:2]
                raw, mix_ref, lengths_ref, table, sems, acc_ref = refs[6:]
                load_and_mix(
                    sz, mix_hbm, lengths_hbm, slices_hbm, left_ref, right_ref, raw, mix_ref, lengths_ref, table, sems
                )
                multiply(sz, piece, left_ref, right_ref, refs[2:6], acc_ref)

            out = chain.call(
                "first",
                body,
                [slice_mix, lengths, slices],
                [((sz.width, sz.depth), jnp.bfloat16), ((sz.depth, sz.extended), jnp.bfloat16)] + shapes,
                scratch=[
                    pltpu.VMEM((sz.count, sz.chunks * sz.chunk, sz.width), jnp.bfloat16),
                    pltpu.SMEM(slice_mix.shape, f32),
                    pltpu.SMEM(lengths.shape, jnp.int32),
                    pltpu.SMEM((2, sz.tiles + 1), jnp.int32),
                    pltpu.SemaphoreType.DMA((sz.chunks + 2,)),
                    acc,
                ],
                specs=[HBM] * 3,
                flops=flops,
                vmem=40,
            )
            state["left"], state["right"] = out[:2]
            out = out[2:]
        else:

            def body(left_ref, right_ref, step_ref, *refs):
                if tail(name):
                    vector(sz, left_ref, right_ref, step_ref, refs[:2])
                multiply(sz, piece, left_ref, right_ref, refs[:4], refs[4])

            out = chain.call(
                "multiply_" + name,
                body,
                [state["left"], state["right"], step_row],
                shapes,
                scratch=[acc],
                flops=flops,
                vmem=40,
            )
        other1, own1, other0, own0 = out
        state[name] = dict(own1=own1, own0=own0, came1=to_core(other1, chips), came0=to_core(other0, chips))

    def first_sum(name):
        s = state[name]
        rows = s["own1"].shape[0]

        def body(own, came, out):
            add_rows(out, 0, rows - tail(name), (own, 0), (came, 0))
            if tail(name):
                add_rows(out, rows - extra, extra, (own, rows - extra), (came, rows - extra))

        s["sent"] = chain.call("sum1_" + name, body, [s["own1"], s["came1"]], [((rows, LANES), f32)])[0]
        s["came"] = across(s["sent"], chips, PIECES[name][1][0])

    def next_sum(name, n):
        s = state[name]
        held = [s["own0"], s["came0"]] if n == 1 else [s["kept"]]
        full = held[0].shape[0]
        rows = full // 2
        more = tail(name)

        def body(*refs):
            own, (sent, came), (send_ref, keep_ref) = refs[:-4], refs[-4:-2], refs[-2:]
            terms = [*own, came]
            add_rows(send_ref, 0, rows, *[(r, rows) for r in terms])
            add_rows(keep_ref, 0, rows, *[(r, 0) for r in terms])
            if more:
                add_rows(send_ref, rows, more, (sent, full), (came, full))

        out = chain.call(
            f"sum{n + 1}_" + name,
            body,
            [*held, s["sent"], s["came"]],
            [((rows + more, LANES), f32), ((rows, LANES), f32)],
        )
        s["sent"], s["kept"] = out
        s["came"] = across(s["sent"], chips, PIECES[name][1][n])

    def finish(name):
        s = state[name]
        shifts = PIECES[name][0]
        rows = s["kept"].shape[0]
        more = tail(name)
        swapped = [k for k in shifts if k and 2 * k != chips]
        shapes = [((sz.parts(k) * unit, LANES), f32) for k in shifts]
        if swapped:
            shapes.append(((len(swapped) * unit, LANES), f32))
        if more:
            shapes.append(((extra, LANES), f32))

        def body(kept, sent, came, *outs):
            at = 0
            for n, k in enumerate(shifts):
                add_rows(outs[n], 0, sz.parts(k) * unit, (kept, at), (came, at))
                if k in swapped:
                    add_rows(outs[len(shifts)], swapped.index(k) * unit, unit, (kept, at + unit), (came, at + unit))
                at += sz.parts(k) * unit
            if more:
                add_rows(outs[-1], 0, extra, (sent, rows), (came, rows))

        out = chain.call("done_" + name, body, [s["kept"], s["sent"], s["came"]], shapes)
        if swapped:
            got = to_core(out[len(shifts)], chips)
        for n, k in enumerate(shifts):
            arrays.append(out[n])
            plan.append(("own" if k else "self", k, 0, len(arrays) - 1, 0))
            if k:
                arrays.append(mirror(out[n], chips, k))
                plan.append(("mirrored", k, 0, len(arrays) - 1, 0))
        if swapped:
            arrays.append(got)
            for n, k in enumerate(swapped):
                plan.append(("swapped", k, n * unit, len(arrays) - 1, 0))
        if more:
            state["step"] = out[-1]

    def join(inputs):
        def body(*refs):
            out_ref = refs[-1]
            chip, core = place()

            def put(device, value):
                out_ref[:, pl.ds(pl.multiple_of(device * unit, unit), unit)] = value

            for kind, k, first, n, _ in plan:
                here = refs[n]
                after, before = lax.rem(chip + k, chips), lax.rem(chip + chips - k, chips)
                top = slice(first, first + unit)
                low = (chip >= k).astype(jnp.int32)
                if kind == "self":
                    for h in range(CORES):
                        put(chip * CORES + (core ^ h), here[h * unit : (h + 1) * unit, :].T)
                elif 2 * k == chips:
                    flip = low if kind == "own" else 1 - low
                    value = here[top, :]
                    put(after * CORES + (core ^ flip), value if kind == "own" else value.T)
                elif kind == "own":
                    put(after * CORES + core, here[top, :])
                elif kind == "swapped":
                    put(after * CORES + 1 - core, here[top, :])
                else:
                    for h in range(CORES):
                        put(before * CORES + (core ^ h), here[h * unit : (h + 1) * unit, :].T)

        return chain.call("join", body, inputs, [((unit, sz.width), f32)])[0]

    arrays, plan = [], []
    for what in ORDER.split():
        if what[0] == "K":
            start(what[1])
        elif what[1] == "1":
            first_sum(what[0])
        elif what[1] == "4":
            finish(what[0])
        else:
            next_sum(what[0], int(what[1]) - 1)
    for name in PIECES:
        if name + "4" not in ORDER:
            finish(name)
    out = join(arrays)
    return out, state["step"].reshape(-1)


def coupled(slices, slice_mix, lengths):
    count = slices.shape[0]
    coupling = (slice_mix + slice_mix.T) * 0.5 * (1.0 - jnp.eye(count, dtype=jnp.float32))
    blocks = lengths.shape[1]
    position = lax.broadcasted_iota(jnp.int32, (blocks, slices.shape[1] // blocks), 1)
    used = (position < lengths[0][:, None]).reshape(-1).astype(jnp.float32)
    out = []
    for k in range(count):
        total = coupling[k, 0] * slices[0].astype(jnp.float32)
        for l in range(1, count):
            total = total + coupling[k, l] * slices[l].astype(jnp.float32)
        out.append(total)
    return (jnp.stack(out) * used[None, :, None]).astype(jnp.bfloat16)


def whole(slices, slice_mix, lengths, search_step):
    width = slices.shape[2]
    left = slices.reshape(-1, width)
    right = coupled(slices, slice_mix, lengths).reshape(-1, width)
    rows = lax.psum_scatter(
        lax.dot_general(left, right, DIMS0, preferred_element_type=jnp.float32), AXIS, scatter_dimension=0, tiled=True
    )
    applied = jnp.dot(right, search_step, preferred_element_type=jnp.float32)
    head = applied.astype(jnp.bfloat16)
    tail = (applied - head.astype(jnp.float32)).astype(jnp.bfloat16)
    share = lax.dot_general(left, head, DIMS0, preferred_element_type=jnp.float32)
    share = share + lax.dot_general(left, tail, DIMS0, preferred_element_type=jnp.float32)
    return rows, lax.psum(share, AXIS)


def solution(mesh):
    devices = mesh.shape[AXIS]

    def on_device(slices, slice_mix, lengths, search_step):
        if fits(devices, slices, lengths):
            return halved(Sizes(devices, slices, lengths), slices, slice_mix, lengths, search_step)
        return whole(slices, slice_mix, lengths, search_step)

    return jax.shard_map(
        on_device,
        mesh=mesh,
        in_specs=(
            P(None, ("groups", AXIS), None),
            P(),
            P(("groups", AXIS), None),
            P("groups"),
        ),
        out_specs=(P(("groups", AXIS), None), P("groups")),
        check_vma=False,
    )
```

```python
import functools

import jax
import jax.numpy as jnp
from jax import lax
from jax.experimental import pallas as pl
from jax.experimental.pallas import tpu as pltpu
from jax.sharding import PartitionSpec as P

AXIS = "block"
CORES = 2
TILE = 16
LANES = 128
DIMS0 = (((0,), (0,)), ((), ()))
DIMS1 = (((1,), (1,)), ((), ()))
VMEM = pl.BlockSpec(memory_space=pltpu.VMEM)
HBM = pl.BlockSpec(memory_space=pltpu.HBM)
ANY = pl.BlockSpec(memory_space=pl.ANY)

PIECES = {
    "a": ((0,), (1, 2, 4)),
    "b": ((1,), (1, 2, 4)),
    "c": ((3,), (2, 4, 1)),
    "d": ((2, 4), (1, 2, 4)),
}
SPLIT = "a"
SWAPPERS = "bcd"
LAST = "a"
CARRIER = "c"
ORDER = (
    *("Ka1", "Kd", "Kb", "Kc", "d1", "Ka0", "V", "c1", "fa", "a1", "b1", "d2", "c2", "b2"),
    *("d3", "a2", "c3", "b3", "d4", "c4", "b4", "a3", "c5", "d5", "b5", "a4", "a5"),
)


class Sizes:
    def __init__(self, devices, slices, lengths):
        self.devices = devices
        self.chips = devices // CORES
        self.count, self.rows, self.width = slices.shape
        self.blocks = lengths.shape[1]
        self.unit = self.width // devices
        self.step = self.rows // self.blocks
        most = self.step // TILE + ((self.blocks - 2) * self.step + (self.blocks - 1) * (TILE - 1)) // TILE
        self.chunk = 256 // self.count
        self.chunks = -(-most * TILE // self.chunk)
        self.tiles = self.chunks * self.chunk // TILE
        self.depth = self.count * self.chunks * self.chunk
        self.extended = self.width + 2 * CORES * self.unit

    def parts(self, shift):
        return 1 if 2 * shift == self.chips else CORES

    def piece_blocks(self, shifts):
        return sum(self.parts(k) for k in shifts)


def fits(devices, slices, lengths):
    unit, step = slices.shape[2] // devices, slices.shape[1] // lengths.shape[1]
    return devices == 16 and unit == LANES and slices.shape[0] == 4 and step % TILE == 0


def place():
    me = lax.axis_index(AXIS)
    return me // CORES, lax.rem(me, CORES)


def load_and_mix(sz, mix_hbm, lengths_hbm, slices_hbm, left_ref, right_ref, raw, mix_ref, lengths_ref, table, sems):
    first = pltpu.make_async_copy(lengths_hbm, lengths_ref, sems.at[sz.chunks])
    second = pltpu.make_async_copy(mix_hbm, mix_ref, sems.at[sz.chunks + 1])
    first.start()
    second.start()
    first.wait()
    for p in range(sz.tiles + 1):
        table[0, p] = 0
        table[1, p] = 0
    at = jnp.int32(0)
    for j in range(sz.blocks):
        for i in range(sz.step // TILE):
            inside = lengths_ref[0, j] - i * TILE
            at_safe = jnp.minimum(at, sz.tiles)
            table[0, at_safe] = jnp.where(inside > 0, j * sz.step + i * TILE, 0)
            table[1, at_safe] = jnp.clip(inside, 0, TILE)
            at = at + (inside > 0).astype(jnp.int32)
    per = sz.chunk // TILE
    for p in range(sz.tiles):
        source = pl.multiple_of(table[0, p], TILE)
        pltpu.make_async_copy(
            slices_hbm.at[:, pl.ds(source, TILE), :], raw.at[:, pl.ds(p * TILE, TILE), :], sems.at[p // per]
        ).start()
    second.wait()
    weight = {}
    for k in range(sz.count):
        for l in range(sz.count):
            if l != k:
                weight[k, l] = (mix_ref[k, l] + mix_ref[l, k]) * 0.5
    unit, wide = sz.unit, CORES * sz.unit
    _, core = place()

    def one_chunk(g, carry):
        here = pl.ds(pl.multiple_of(g * sz.chunk, sz.chunk), sz.chunk)
        pltpu.make_async_copy(slices_hbm.at[:, pl.ds(0, sz.chunk), :], raw.at[:, here, :], sems.at[g]).wait()
        base = g * sz.count * sz.chunk
        row = lax.broadcasted_iota(jnp.int32, (TILE, unit), 0)
        used = [row < table[1, g * per + p] for p in range(per)]

        def one_chip(i, carry):
            for c in range(CORES):
                cols = pl.ds(pl.multiple_of(i * wide + c * unit, unit), unit)
                mine = pl.ds(pl.multiple_of(i * wide + (c ^ core) * unit, unit), unit)
                for p in range(per):
                    rows = pl.ds(pl.multiple_of(g * sz.chunk + p * TILE, TILE), TILE)
                    f = [raw[k, rows, cols].astype(jnp.float32) for k in range(sz.count)]
                    for k in range(sz.count):
                        total = None
                        for l in range(sz.count):
                            if l != k:
                                term = weight[k, l] * f[l]
                                total = term if total is None else total + term
                        to = pl.ds(pl.multiple_of(base + k * sz.chunk + p * TILE, TILE), TILE)
                        right_ref[to, mine] = jnp.where(used[p], total, 0.0).astype(jnp.bfloat16)
                block = raw[:, here, cols].reshape(sz.count * sz.chunk, unit)
                left_ref[mine, pl.ds(pl.multiple_of(base, LANES), sz.count * sz.chunk)] = block.T
            return carry

        lax.fori_loop(0, sz.chips, one_chip, 0)
        rows = pl.ds(pl.multiple_of(base, LANES), sz.count * sz.chunk)
        right_ref[rows, sz.width :] = right_ref[rows, : sz.extended - sz.width]
        return carry

    lax.fori_loop(0, sz.chunks, one_chunk, 0)


def runs(shifts):
    out = []
    for k in shifts:
        if out and out[-1][-1] + 1 == k:
            out[-1].append(k)
        else:
            out.append([k])
    return out


def multiply(sz, piece, bit, left_ref, right_ref, other_ref, own_ref, first=0):
    shifts, order = piece
    unit, chips = sz.unit, sz.chips
    blocks = sz.piece_blocks(shifts)
    wide = CORES * unit
    chip, _ = place()
    half = chips // 2
    for index in range(half):
        slot = bit * order[0]
        for n, mask in enumerate(order[1:]):
            slot += mask * ((index >> (len(order) - 2 - n)) & 1)
        row = chip ^ slot
        at = first // unit + index * blocks
        for run in runs(shifts):
            col = lax.rem(row + run[0], chips)
            tile = jnp.dot(
                left_ref[pl.ds(pl.multiple_of(row * wide, wide), wide), :],
                right_ref[:, pl.ds(pl.multiple_of(col * wide, wide), wide * len(run))],
                preferred_element_type=jnp.float32,
            )
            for n, k in enumerate(run):
                for ref, owner in ((own_ref, 0), (other_ref, 1)):
                    if 2 * k == chips:
                        rows = tile[owner * unit : (owner + 1) * unit, n * wide : (n + 1) * wide]
                        same, cross = (rows[:, (owner ^ f) * unit : ((owner ^ f) + 1) * unit] for f in (0, 1))
                        ref[at * unit : (at + 1) * unit, :] = jnp.where(row >= half, cross, same)
                    else:
                        left = n * wide + owner * unit
                        for h in range(CORES):
                            rows = owner ^ h
                            ref[(at + h) * unit : (at + h + 1) * unit, :] = tile[
                                rows * unit : (rows + 1) * unit, left : left + unit
                            ]
                at += sz.parts(k)


def vector(sz, left_ref, right_ref, step_ref, outs):
    unit = sz.unit
    _, core = place()
    turned = []
    for d in range(sz.devices):
        turned.append(step_ref[:, pl.ds(pl.multiple_of((d ^ core) * unit, unit), unit)])
    x = jnp.broadcast_to(jnp.concatenate(turned, axis=1), (8, sz.width))
    applied = lax.dot_general(x, right_ref[:, : sz.width], DIMS1, preferred_element_type=jnp.float32)
    head = applied.astype(jnp.bfloat16).astype(jnp.float32)
    row = lax.broadcasted_iota(jnp.int32, applied.shape, 0)
    both = jnp.where(row == 0, head, jnp.where(row == 1, applied - head, 0.0)).astype(jnp.bfloat16)
    share = lax.dot_general(both, left_ref[...], DIMS1, preferred_element_type=jnp.float32)
    share = share[0:1, :] + share[1:2, :]
    for ref in outs:
        first = ref.shape[0] - sz.devices
        for d in range(sz.devices):
            ref[pl.ds(first + (d ^ core), 1), :] = share[:, d * unit : (d + 1) * unit]


def add_rows(to, at, size, *terms):
    block = LANES if size % LANES == 0 else size

    def one(i, carry):
        total = None
        for ref, first in terms:
            value = ref[pl.ds(pl.multiple_of(first + i * block, 8), block), :]
            total = value if total is None else total + value
        to[pl.ds(pl.multiple_of(at + i * block, 8), block), :] = total
        return carry

    lax.fori_loop(0, size // block, one, 0)


class Chain:
    def __init__(self):
        self.token = None

    def call(self, name, body, inputs, shapes, scratch=(), specs=None, outs=None, alias=None, flops=0, vmem=4):
        specs = list(specs or [VMEM] * len(inputs))
        inputs = list(inputs)
        count = len(inputs)
        if self.token is not None:
            inputs.append(self.token)
            specs.append(ANY)

        def kernel(*refs):
            body(*refs[:count], *refs[len(inputs) :])

        out = pl.pallas_call(
            kernel,
            in_specs=specs,
            out_specs=outs or [VMEM] * len(shapes),
            input_output_aliases=alias or {},
            out_shape=[jax.ShapeDtypeStruct(s, d) for s, d in shapes],
            scratch_shapes=list(scratch),
            cost_estimate=pl.CostEstimate(flops=flops, bytes_accessed=0, transcendentals=0),
            compiler_params=pltpu.CompilerParams(vmem_limit_bytes=vmem << 20),
            name=name,
        )(*inputs)
        self.token = out[-1]
        return out


def send(x, chips, to):
    pairs = []
    for chip in range(chips):
        for core in range(CORES):
            other, its_core = to(chip, core)
            pairs.append((chip * CORES + core, other * CORES + its_core))
    return lax.ppermute(x, AXIS, pairs)


def to_core(x, chips):
    return send(x, chips, lambda m, c: (m, 1 - c))


def across(x, chips, mask):
    return send(x, chips, lambda m, c: (m ^ mask, c))


def mirror(x, chips, shift):
    def to(m, c):
        flip = int(m >= shift) if 2 * shift == chips else 0
        return (m + shift) % chips, c ^ flip

    return send(x, chips, to)


def halved(sz, slices, slice_mix, lengths, search_step):
    chips, unit, f32 = sz.chips, sz.unit, jnp.float32
    chain = Chain()
    extra = sz.width // LANES
    state = {"swaps": []}
    step_row = search_step.reshape(1, -1)

    def tail(name):
        return extra if name == CARRIER else 0

    def start(name, bits):
        piece = PIECES[name]
        shifts = piece[0]
        half = chips // 2 * sz.piece_blocks(shifts) * unit
        rows = half * len(bits)
        shapes = [((rows, LANES), f32)] * 2
        flops = chips * (CORES * unit) ** 2 * len(shifts) * sz.depth * len(bits)
        if "left" not in state:

            def body(mix_hbm, lengths_hbm, slices_hbm, left_ref, right_ref, other_ref, own_ref, *scratch):
                load_and_mix(sz, mix_hbm, lengths_hbm, slices_hbm, left_ref, right_ref, *scratch)
                multiply(sz, piece, bits[0], left_ref, right_ref, other_ref, own_ref)

            out = chain.call(
                "first",
                body,
                [pltpu.with_memory_space_constraint(a, pltpu.HBM) for a in (slice_mix, lengths, slices)],
                [((sz.width, sz.depth), jnp.bfloat16), ((sz.depth, sz.extended), jnp.bfloat16)] + shapes,
                scratch=[
                    pltpu.VMEM((sz.count, sz.chunks * sz.chunk, sz.width), jnp.bfloat16),
                    pltpu.SMEM(slice_mix.shape, f32),
                    pltpu.SMEM(lengths.shape, jnp.int32),
                    pltpu.SMEM((2, sz.tiles + 1), jnp.int32),
                    pltpu.SemaphoreType.DMA((sz.chunks + 2,)),
                ],
                specs=[HBM] * 3,
                flops=flops,
                vmem=12,
            )
            state["left"], state["right"] = out[:2]
            other, own = out[2:]
        else:

            def body(left_ref, right_ref, other_ref, own_ref):
                for n, bit in enumerate(bits):
                    multiply(sz, piece, bit, left_ref, right_ref, other_ref, own_ref, n * half)

            other, own = chain.call(
                "multiply_" + name,
                body,
                [state["left"], state["right"]],
                shapes,
                flops=flops,
                vmem=8,
            )
        s = state.setdefault(name, {})
        n = bits[0] if len(bits) == 1 else ""
        s[f"own{n}"], s[f"came{n}"] = own, to_core(other, chips)

    def start_vector():
        def body(left_ref, right_ref, step_ref, out_ref):
            vector(sz, left_ref, right_ref, step_ref, [out_ref])

        share = chain.call(
            "vector", body, [state["left"], state["right"], step_row], [((extra, LANES), f32)], vmem=8
        )[0]
        state["vector"] = [share, to_core(share, chips)]

    def first_sum(name):
        s = state[name]
        half = chips // 2 * sz.piece_blocks(PIECES[name][0]) * unit
        more = tail(name)
        if name in SPLIT:

            def body(own, came, out):
                add_rows(out, 0, half, (own, 0), (came, 0))

            s["sent"] = chain.call("sum1_" + name, body, [s["own1"], s["came1"]], [((half, LANES), f32)])[0]
        else:

            def body(own, came, *refs):
                send_ref, keep_ref = refs[-2:]
                add_rows(send_ref, 0, half, (own, 0), (came, 0))
                add_rows(keep_ref, 0, half, (own, half), (came, half))
                if more:
                    add_rows(send_ref, half, more, (refs[0], 0), (refs[1], 0))

            s["sent"], s["kept"] = chain.call(
                "sum1_" + name,
                body,
                [s["own"], s["came"], *(state["vector"] if more else [])],
                [((half + more, LANES), f32), ((half, LANES), f32)],
            )
        s["came"] = across(s["sent"], chips, PIECES[name][1][0])

    def fold(name):
        s = state[name]
        rows = s["own0"].shape[0]

        def body(own, came, out):
            add_rows(out, 0, rows, (own, 0), (came, 0))

        s["kept"] = chain.call("fold_" + name, body, [s["own0"], s["came0"]], [((rows, LANES), f32)])[0]

    def next_sum(name, n):
        s = state[name]
        shifts, order = PIECES[name]
        full = s["kept"].shape[0]
        rows = full // 2
        more = tail(name)
        half = first_row(shifts, chips // 2) if n == len(order) - 1 and chips // 2 in shifts else None
        both = 0 if half is None else unit

        def body(kept, sent, came, send_ref, keep_ref):
            add_rows(send_ref, 0, rows, (kept, rows), (came, rows))
            add_rows(keep_ref, 0, rows, (kept, 0), (came, 0))
            if both:
                add_rows(send_ref, rows, both, (kept, half), (came, half))
            if more:
                add_rows(send_ref, rows + both, more, (sent, full), (came, full))

        s["sent"], s["kept"] = chain.call(
            f"sum{n + 1}_" + name,
            body,
            [s["kept"], s["sent"], s["came"]],
            [((rows + both + more, LANES), f32), ((rows, LANES), f32)],
        )
        s["came"] = across(s["sent"], chips, order[n])

    def first_row(shifts, shift):
        return unit * sz.piece_blocks([k for k in shifts if k < shift])

    def finish(name):
        s = state[name]
        shifts = PIECES[name][0]
        rows = s["kept"].shape[0]
        more = tail(name)
        swapped = [k for k in shifts if k]
        last = name in SWAPPERS
        before = list(state["swaps"]) if last else []
        shapes = [((CORES * unit, LANES), f32) for k in shifts]
        if last:
            shapes.append((((len(swapped) + len(before)) * unit, LANES), f32))
        if more:
            shapes.append(((extra, LANES), f32))

        def body(kept, sent, came, *refs):
            outs = refs[len(before) :]
            for n, k in enumerate(shifts):
                at = first_row(shifts, k)
                terms = [((kept, at + h * unit), (came, at + h * unit)) for h in range(sz.parts(k))]
                if 2 * k == chips:
                    terms.append(((sent, at), (came, rows)))
                for h, pair in enumerate(terms):
                    add_rows(outs[n], h * unit, unit, *pair)
                if last and k in swapped:
                    add_rows(outs[len(shifts)], (len(before) + swapped.index(k)) * unit, unit, *terms[1])
            for n, (_, _, row, _) in enumerate(before):
                add_rows(outs[len(shifts)], n * unit, unit, (refs[n], row))
            if more:
                add_rows(outs[-1], 0, extra, (sent, rows), (came, rows))

        out = chain.call("done_" + name, body, [s["kept"], s["sent"], s["came"], *(b[0] for b in before)], shapes)
        s["done"] = list(out[: len(shifts)])
        s["plan"] = [(k, "own", n, 0) for n, k in enumerate(shifts)]
        for k in swapped:
            if 2 * k != chips:
                s["plan"].append((k, "mirrored", len(s["done"]), 0))
                s["done"].append(mirror(out[shifts.index(k)], chips, k))
        for n, k in enumerate(swapped):
            state["swaps"].append((out[shifts.index(k)], k, unit, name))
        if last:
            for n, (_, k, _, _) in enumerate(state["swaps"]):
                s["plan"].append((k, "swapped", len(s["done"]), n * unit))
            s["done"].append(to_core(out[len(shifts)], chips))
            state["swaps"] = []
        if more:
            state["step"] = out[-1]

    def place_blocks(name):
        s = state[name]
        inputs, plan = s["done"], s["plan"]
        old = [state["out"]] if "out" in state else []
        final = name == LAST

        def body(*refs):
            chip, core = place()
            to = refs[len(inputs)]

            def put(device, value):
                to[:, pl.ds(pl.multiple_of(device * unit, unit), unit)] = value

            for k, kind, n, first in plan:
                here = refs[n]
                after, before = lax.rem(chip + k, chips), lax.rem(chip + chips - k, chips)
                one, two = (slice(first + h * unit, first + (h + 1) * unit) for h in range(2))
                low = (chip >= k).astype(jnp.int32)
                if k == 0:
                    put(chip * CORES + core, here[one, :].T)
                    put(chip * CORES + 1 - core, here[two, :].T)
                elif 2 * k == chips and kind == "own":
                    put(after * CORES + (core ^ low), here[one, :])
                    mine = (here, two)
                elif 2 * k == chips:
                    value = jnp.where(low > 0, mine[0][mine[1], :], here[one, :])
                    put(after * CORES + (core ^ (1 - low)), value.T)
                elif kind == "own":
                    put(after * CORES + core, here[one, :])
                elif kind == "swapped":
                    put(after * CORES + 1 - core, here[one, :])
                else:
                    put(before * CORES + core, here[one, :].T)
                    put(before * CORES + 1 - core, here[two, :].T)
            if final:
                pltpu.sync_copy(to, refs[len(inputs) + 1])

        state["out"] = chain.call(
            "place_" + name,
            body,
            [*inputs, *old],
            [((unit, sz.width), f32)],
            outs=[HBM] if final else [VMEM],
            alias={len(inputs): 0} if old and not final else None,
        )[0]

    for what in ORDER:
        if what == "V":
            start_vector()
        elif what[0] == "K":
            start(what[1], (int(what[2]),) if what[2:] else (1, 0))
        elif what[0] == "f":
            fold(what[1])
        elif what[1] == "1":
            first_sum(what[0])
        elif what[1] == "4":
            finish(what[0])
        elif what[1] == "5":
            place_blocks(what[0])
        else:
            next_sum(what[0], int(what[1]) - 1)
    return state["out"], state["step"].reshape(-1)


def coupled(slices, slice_mix, lengths):
    count = slices.shape[0]
    coupling = (slice_mix + slice_mix.T) * 0.5 * (1.0 - jnp.eye(count, dtype=jnp.float32))
    blocks = lengths.shape[1]
    position = lax.broadcasted_iota(jnp.int32, (blocks, slices.shape[1] // blocks), 1)
    used = (position < lengths[0][:, None]).reshape(-1).astype(jnp.float32)
    out = []
    for k in range(count):
        total = coupling[k, 0] * slices[0].astype(jnp.float32)
        for l in range(1, count):
            total = total + coupling[k, l] * slices[l].astype(jnp.float32)
        out.append(total)
    return (jnp.stack(out) * used[None, :, None]).astype(jnp.bfloat16)


def whole(slices, slice_mix, lengths, search_step):
    width = slices.shape[2]
    left = slices.reshape(-1, width)
    right = coupled(slices, slice_mix, lengths).reshape(-1, width)
    rows = lax.psum_scatter(
        lax.dot_general(left, right, DIMS0, preferred_element_type=jnp.float32), AXIS, scatter_dimension=0, tiled=True
    )
    applied = jnp.dot(right, search_step, preferred_element_type=jnp.float32)
    head = applied.astype(jnp.bfloat16)
    tail = (applied - head.astype(jnp.float32)).astype(jnp.bfloat16)
    share = lax.dot_general(left, head, DIMS0, preferred_element_type=jnp.float32)
    share = share + lax.dot_general(left, tail, DIMS0, preferred_element_type=jnp.float32)
    return rows, lax.psum(share, AXIS)


def solution(mesh):
    devices = mesh.shape[AXIS]

    def on_device(slices, slice_mix, lengths, search_step):
        if fits(devices, slices, lengths):
            return halved(Sizes(devices, slices, lengths), slices, slice_mix, lengths, search_step)
        return whole(slices, slice_mix, lengths, search_step)

    return jax.shard_map(
        on_device,
        mesh=mesh,
        in_specs=(
            P(None, ("groups", AXIS), None),
            P(),
            P(("groups", AXIS), None),
            P("groups"),
        ),
        out_specs=(P(("groups", AXIS), None), P("groups")),
        check_vma=False,
    )
```

```python
import functools

import jax
import jax.numpy as jnp
from jax import lax
from jax.experimental import pallas as pl
from jax.experimental.pallas import tpu as pltpu
from jax.sharding import PartitionSpec as P

AXIS = "block"
CORES = 2
TILE = 16
LANES = 128
DIMS0 = (((0,), (0,)), ((), ()))
DIMS1 = (((1,), (1,)), ((), ()))
VMEM = pl.BlockSpec(memory_space=pltpu.VMEM)
HBM = pl.BlockSpec(memory_space=pltpu.HBM)
ANY = pl.BlockSpec(memory_space=pl.ANY)

PIECES = {
    "a": ((0,), (1, 2, 4)),
    "b": ((2,), (2, 4, 1)),
    "c": ((3,), (1, 2, 4)),
    "d": ((1, 4), (1, 2, 4)),
}
SPLIT = "abcd"
SWAPPERS = "bcd"
LAST = "a"
CARRIER = "c"
ORDER = (
    *("Kd1", "Kb1", "Ka1", "d1", "Kd0", "a1", "b1", "Kb0", "Ka0", "Kc1", "fb", "fa", "V", "fd"),
    *("Kc0", "c1", "d2", "b2", "fc", "d3", "c2", "b3", "a2", "c3", "d4", "b4", "a3", "c4"),
    *("d5", "b5", "c5", "a4", "a5"),
)


class Sizes:
    def __init__(self, devices, slices, lengths):
        self.devices = devices
        self.chips = devices // CORES
        self.count, self.rows, self.width = slices.shape
        self.blocks = lengths.shape[1]
        self.unit = self.width // devices
        self.step = self.rows // self.blocks
        most = self.step // TILE + ((self.blocks - 2) * self.step + (self.blocks - 1) * (TILE - 1)) // TILE
        self.chunk = 256 // self.count
        self.chunks = -(-most * TILE // self.chunk)
        self.tiles = self.chunks * self.chunk // TILE
        self.depth = self.count * self.chunks * self.chunk
        self.extended = self.width + 2 * CORES * self.unit

    def parts(self, shift):
        return 1 if 2 * shift == self.chips else CORES

    def piece_blocks(self, shifts):
        return sum(self.parts(k) for k in shifts)


def fits(devices, slices, lengths):
    unit, step = slices.shape[2] // devices, slices.shape[1] // lengths.shape[1]
    return devices == 16 and unit == LANES and slices.shape[0] == 4 and step % TILE == 0


def place():
    me = lax.axis_index(AXIS)
    return me // CORES, lax.rem(me, CORES)


def load_and_mix(sz, mix_hbm, lengths_hbm, slices_hbm, left_ref, right_ref, raw, mix_ref, lengths_ref, table, sems):
    first = pltpu.make_async_copy(lengths_hbm, lengths_ref, sems.at[sz.chunks])
    second = pltpu.make_async_copy(mix_hbm, mix_ref, sems.at[sz.chunks + 1])
    first.start()
    second.start()
    first.wait()
    for p in range(sz.tiles + 1):
        table[0, p] = 0
        table[1, p] = 0
    at = jnp.int32(0)
    for j in range(sz.blocks):
        for i in range(sz.step // TILE):
            inside = lengths_ref[0, j] - i * TILE
            at_safe = jnp.minimum(at, sz.tiles)
            table[0, at_safe] = jnp.where(inside > 0, j * sz.step + i * TILE, 0)
            table[1, at_safe] = jnp.clip(inside, 0, TILE)
            at = at + (inside > 0).astype(jnp.int32)
    per = sz.chunk // TILE
    for p in range(sz.tiles):
        source = pl.multiple_of(table[0, p], TILE)
        pltpu.make_async_copy(
            slices_hbm.at[:, pl.ds(source, TILE), :], raw.at[:, pl.ds(p * TILE, TILE), :], sems.at[p // per]
        ).start()
    second.wait()
    weight = {}
    for k in range(sz.count):
        for l in range(sz.count):
            if l != k:
                weight[k, l] = (mix_ref[k, l] + mix_ref[l, k]) * 0.5
    unit, wide = sz.unit, CORES * sz.unit
    _, core = place()

    def one_chunk(g, carry):
        here = pl.ds(pl.multiple_of(g * sz.chunk, sz.chunk), sz.chunk)
        pltpu.make_async_copy(slices_hbm.at[:, pl.ds(0, sz.chunk), :], raw.at[:, here, :], sems.at[g]).wait()
        base = g * sz.count * sz.chunk
        row = lax.broadcasted_iota(jnp.int32, (TILE, unit), 0)
        used = [row < table[1, g * per + p] for p in range(per)]

        def one_chip(i, carry):
            for c in range(CORES):
                cols = pl.ds(pl.multiple_of(i * wide + c * unit, unit), unit)
                mine = pl.ds(pl.multiple_of(i * wide + (c ^ core) * unit, unit), unit)
                for p in range(per):
                    rows = pl.ds(pl.multiple_of(g * sz.chunk + p * TILE, TILE), TILE)
                    f = [raw[k, rows, cols].astype(jnp.float32) for k in range(sz.count)]
                    for k in range(sz.count):
                        total = None
                        for l in range(sz.count):
                            if l != k:
                                term = weight[k, l] * f[l]
                                total = term if total is None else total + term
                        to = pl.ds(pl.multiple_of(base + k * sz.chunk + p * TILE, TILE), TILE)
                        right_ref[to, mine] = jnp.where(used[p], total, 0.0).astype(jnp.bfloat16)
                block = raw[:, here, cols].reshape(sz.count * sz.chunk, unit)
                left_ref[mine, pl.ds(pl.multiple_of(base, LANES), sz.count * sz.chunk)] = block.T
            return carry

        lax.fori_loop(0, sz.chips, one_chip, 0)
        rows = pl.ds(pl.multiple_of(base, LANES), sz.count * sz.chunk)
        right_ref[rows, sz.width :] = right_ref[rows, : sz.extended - sz.width]
        return carry

    lax.fori_loop(0, sz.chunks, one_chunk, 0)


def runs(shifts):
    out = []
    for k in shifts:
        if out and out[-1][-1] + 1 == k:
            out[-1].append(k)
        else:
            out.append([k])
    return out


def multiply(sz, piece, bit, left_ref, right_ref, other_ref, own_ref, first=0):
    shifts, order = piece
    unit, chips = sz.unit, sz.chips
    blocks = sz.piece_blocks(shifts)
    wide = CORES * unit
    chip, _ = place()
    half = chips // 2
    for index in range(half):
        slot = bit * order[0]
        for n, mask in enumerate(order[1:]):
            slot += mask * ((index >> (len(order) - 2 - n)) & 1)
        row = chip ^ slot
        at = first // unit + index * blocks
        for run in runs(shifts):
            col = lax.rem(row + run[0], chips)
            tile = jnp.dot(
                left_ref[pl.ds(pl.multiple_of(row * wide, wide), wide), :],
                right_ref[:, pl.ds(pl.multiple_of(col * wide, wide), wide * len(run))],
                preferred_element_type=jnp.float32,
            )
            for n, k in enumerate(run):
                for ref, owner in ((own_ref, 0), (other_ref, 1)):
                    if 2 * k == chips:
                        rows = tile[owner * unit : (owner + 1) * unit, n * wide : (n + 1) * wide]
                        same, cross = (rows[:, (owner ^ f) * unit : ((owner ^ f) + 1) * unit] for f in (0, 1))
                        ref[at * unit : (at + 1) * unit, :] = jnp.where(row >= half, cross, same)
                    else:
                        left = n * wide + owner * unit
                        for h in range(CORES):
                            rows = owner ^ h
                            ref[(at + h) * unit : (at + h + 1) * unit, :] = tile[
                                rows * unit : (rows + 1) * unit, left : left + unit
                            ]
                at += sz.parts(k)


def vector(sz, left_ref, right_ref, step_ref, outs):
    unit = sz.unit
    _, core = place()
    turned = []
    for d in range(sz.devices):
        turned.append(step_ref[:, pl.ds(pl.multiple_of((d ^ core) * unit, unit), unit)])
    x = jnp.broadcast_to(jnp.concatenate(turned, axis=1), (8, sz.width))
    applied = lax.dot_general(x, right_ref[:, : sz.width], DIMS1, preferred_element_type=jnp.float32)
    head = applied.astype(jnp.bfloat16).astype(jnp.float32)
    row = lax.broadcasted_iota(jnp.int32, applied.shape, 0)
    both = jnp.where(row == 0, head, jnp.where(row == 1, applied - head, 0.0)).astype(jnp.bfloat16)
    share = lax.dot_general(both, left_ref[...], DIMS1, preferred_element_type=jnp.float32)
    share = share[0:1, :] + share[1:2, :]
    for ref in outs:
        first = ref.shape[0] - sz.devices
        for d in range(sz.devices):
            ref[pl.ds(first + (d ^ core), 1), :] = share[:, d * unit : (d + 1) * unit]


def add_rows(to, at, size, *terms):
    block = LANES if size % LANES == 0 else size

    def one(i, carry):
        total = None
        for ref, first in terms:
            value = ref[pl.ds(pl.multiple_of(first + i * block, 8), block), :]
            total = value if total is None else total + value
        to[pl.ds(pl.multiple_of(at + i * block, 8), block), :] = total
        return carry

    lax.fori_loop(0, size // block, one, 0)


class Chain:
    def __init__(self):
        self.token = None

    def call(self, name, body, inputs, shapes, scratch=(), specs=None, outs=None, alias=None, flops=0, vmem=4):
        specs = list(specs or [VMEM] * len(inputs))
        inputs = list(inputs)
        count = len(inputs)
        if self.token is not None:
            inputs.append(self.token)
            specs.append(ANY)

        def kernel(*refs):
            body(*refs[:count], *refs[len(inputs) :])

        out = pl.pallas_call(
            kernel,
            in_specs=specs,
            out_specs=outs or [VMEM] * len(shapes),
            input_output_aliases=alias or {},
            out_shape=[jax.ShapeDtypeStruct(s, d) for s, d in shapes],
            scratch_shapes=list(scratch),
            cost_estimate=pl.CostEstimate(flops=flops, bytes_accessed=0, transcendentals=0),
            compiler_params=pltpu.CompilerParams(vmem_limit_bytes=vmem << 20),
            name=name,
        )(*inputs)
        self.token = out[0]
        return out


def send(x, chips, to):
    pairs = []
    for chip in range(chips):
        for core in range(CORES):
            other, its_core = to(chip, core)
            pairs.append((chip * CORES + core, other * CORES + its_core))
    return lax.ppermute(x, AXIS, pairs)


def to_core(x, chips):
    return send(x, chips, lambda m, c: (m, 1 - c))


def across(x, chips, mask):
    return send(x, chips, lambda m, c: (m ^ mask, c))


def mirror(x, chips, shift):
    def to(m, c):
        flip = int(m >= shift) if 2 * shift == chips else 0
        return (m + shift) % chips, c ^ flip

    return send(x, chips, to)


def halved(sz, slices, slice_mix, lengths, search_step):
    chips, unit, f32 = sz.chips, sz.unit, jnp.float32
    chain = Chain()
    extra = sz.width // LANES
    state = {"swaps": []}
    step_row = search_step.reshape(1, -1)

    def tail(name):
        return extra if name == CARRIER else 0

    def start(name, bits):
        piece = PIECES[name]
        shifts = piece[0]
        half = chips // 2 * sz.piece_blocks(shifts) * unit
        rows = half * len(bits)
        shapes = [((rows, LANES), f32)] * 2
        flops = chips * (CORES * unit) ** 2 * len(shifts) * sz.depth * len(bits)
        if "left" not in state:

            def body(mix_hbm, lengths_hbm, slices_hbm, left_ref, right_ref, other_ref, own_ref, *scratch):
                load_and_mix(sz, mix_hbm, lengths_hbm, slices_hbm, left_ref, right_ref, *scratch)
                multiply(sz, piece, bits[0], left_ref, right_ref, other_ref, own_ref)

            out = chain.call(
                "first",
                body,
                [pltpu.with_memory_space_constraint(a, pltpu.HBM) for a in (slice_mix, lengths, slices)],
                [((sz.width, sz.depth), jnp.bfloat16), ((sz.depth, sz.extended), jnp.bfloat16)] + shapes,
                scratch=[
                    pltpu.VMEM((sz.count, sz.chunks * sz.chunk, sz.width), jnp.bfloat16),
                    pltpu.SMEM(slice_mix.shape, f32),
                    pltpu.SMEM(lengths.shape, jnp.int32),
                    pltpu.SMEM((2, sz.tiles + 1), jnp.int32),
                    pltpu.SemaphoreType.DMA((sz.chunks + 2,)),
                ],
                specs=[HBM] * 3,
                flops=flops,
                vmem=12,
            )
            state["left"], state["right"] = out[:2]
            other, own = out[2:]
        else:

            def body(left_ref, right_ref, other_ref, own_ref):
                for n, bit in enumerate(bits):
                    multiply(sz, piece, bit, left_ref, right_ref, other_ref, own_ref, n * half)

            other, own = chain.call(
                "multiply_" + name,
                body,
                [state["left"], state["right"]],
                shapes,
                flops=flops,
                vmem=8,
            )
        s = state.setdefault(name, {})
        n = bits[0] if len(bits) == 1 else ""
        s[f"own{n}"], s[f"came{n}"] = own, to_core(other, chips)

    def start_vector():
        def body(left_ref, right_ref, step_ref, out_ref):
            vector(sz, left_ref, right_ref, step_ref, [out_ref])

        share = chain.call(
            "vector", body, [state["left"], state["right"], step_row], [((extra, LANES), f32)], vmem=8
        )[0]
        state["vector"] = [share, to_core(share, chips)]

    def first_sum(name):
        s = state[name]
        half = chips // 2 * sz.piece_blocks(PIECES[name][0]) * unit
        more = tail(name)
        if name in SPLIT:

            def body(own, came, *refs):
                add_rows(refs[-1], 0, half, (own, 0), (came, 0))
                if more:
                    add_rows(refs[-1], half, more, (refs[0], 0), (refs[1], 0))

            inputs = [s["own1"], s["came1"], *(state["vector"] if more else [])]
            s["sent"] = chain.call("sum1_" + name, body, inputs, [((half + more, LANES), f32)])[0]
        else:

            def body(own, came, *refs):
                send_ref, keep_ref = refs[-2:]
                add_rows(send_ref, 0, half, (own, 0), (came, 0))
                add_rows(keep_ref, 0, half, (own, half), (came, half))
                if more:
                    add_rows(send_ref, half, more, (refs[0], 0), (refs[1], 0))

            s["sent"], s["kept"] = chain.call(
                "sum1_" + name,
                body,
                [s["own"], s["came"], *(state["vector"] if more else [])],
                [((half + more, LANES), f32), ((half, LANES), f32)],
            )
        s["came"] = across(s["sent"], chips, PIECES[name][1][0])

    def fold(name):
        s = state[name]
        rows = s["own0"].shape[0]

        def body(own, came, out):
            add_rows(out, 0, rows, (own, 0), (came, 0))

        s["kept"] = chain.call("fold_" + name, body, [s["own0"], s["came0"]], [((rows, LANES), f32)])[0]

    def next_sum(name, n):
        s = state[name]
        shifts, order = PIECES[name]
        full = s["kept"].shape[0]
        rows = full // 2
        more = tail(name)
        half = first_row(shifts, chips // 2) if n == len(order) - 1 and chips // 2 in shifts else None
        both = 0 if half is None else unit

        def body(kept, sent, came, send_ref, keep_ref):
            add_rows(send_ref, 0, rows, (kept, rows), (came, rows))
            add_rows(keep_ref, 0, rows, (kept, 0), (came, 0))
            if both:
                add_rows(send_ref, rows, both, (kept, half), (came, half))
            if more:
                add_rows(send_ref, rows + both, more, (sent, full), (came, full))

        s["sent"], s["kept"] = chain.call(
            f"sum{n + 1}_" + name,
            body,
            [s["kept"], s["sent"], s["came"]],
            [((rows + both + more, LANES), f32), ((rows, LANES), f32)],
        )
        s["came"] = across(s["sent"], chips, order[n])

    def first_row(shifts, shift):
        return unit * sz.piece_blocks([k for k in shifts if k < shift])

    def finish(name):
        s = state[name]
        shifts = PIECES[name][0]
        rows = s["kept"].shape[0]
        more = tail(name)
        swapped = [k for k in shifts if k]
        last = name in SWAPPERS
        before = list(state["swaps"]) if last else []
        shapes = [((CORES * unit, LANES), f32) for k in shifts]
        if last:
            shapes.append((((len(swapped) + len(before)) * unit, LANES), f32))
        if more:
            shapes.append(((extra, LANES), f32))

        def body(kept, sent, came, *refs):
            outs = refs[len(before) :]
            for n, k in enumerate(shifts):
                at = first_row(shifts, k)
                terms = [((kept, at + h * unit), (came, at + h * unit)) for h in range(sz.parts(k))]
                if 2 * k == chips:
                    terms.append(((sent, at), (came, rows)))
                for h, pair in enumerate(terms):
                    add_rows(outs[n], h * unit, unit, *pair)
                if last and k in swapped:
                    add_rows(outs[len(shifts)], (len(before) + swapped.index(k)) * unit, unit, *terms[1])
            for n, (_, _, row, _) in enumerate(before):
                add_rows(outs[len(shifts)], n * unit, unit, (refs[n], row))
            if more:
                add_rows(outs[-1], 0, extra, (sent, rows), (came, rows))

        out = chain.call("done_" + name, body, [s["kept"], s["sent"], s["came"], *(b[0] for b in before)], shapes)
        s["done"] = list(out[: len(shifts)])
        s["plan"] = [(k, "own", n, 0) for n, k in enumerate(shifts)]
        for k in swapped:
            if 2 * k != chips:
                s["plan"].append((k, "mirrored", len(s["done"]), 0))
                s["done"].append(mirror(out[shifts.index(k)], chips, k))
        for n, k in enumerate(swapped):
            state["swaps"].append((out[shifts.index(k)], k, unit, name))
        if last:
            for n, (_, k, _, _) in enumerate(state["swaps"]):
                s["plan"].append((k, "swapped", len(s["done"]), n * unit))
            s["done"].append(to_core(out[len(shifts)], chips))
            state["swaps"] = []
        if more:
            state["step"] = out[-1]

    def place_blocks(name):
        s = state[name]
        inputs, plan = s["done"], s["plan"]
        old = [state["out"]] if "out" in state else []

        def body(*refs):
            chip, core = place()
            to = refs[len(inputs) + len(old)]

            def put(device, value):
                to[:, pl.ds(pl.multiple_of(device * unit, unit), unit)] = value

            for k, kind, n, first in plan:
                here = refs[n]
                after, before = lax.rem(chip + k, chips), lax.rem(chip + chips - k, chips)
                one, two = (slice(first + h * unit, first + (h + 1) * unit) for h in range(2))
                low = (chip >= k).astype(jnp.int32)
                if 2 * k == chips and kind == "own":
                    put(after * CORES + (core ^ low), here[one, :])
                    mine = (here, two)
                elif 2 * k == chips:
                    value = jnp.where(low > 0, mine[0][mine[1], :], here[one, :])
                    put(after * CORES + (core ^ (1 - low)), value.T)
                elif kind == "own":
                    put(after * CORES + core, here[one, :])
                elif kind == "swapped":
                    put(after * CORES + 1 - core, here[one, :])
                else:
                    put(before * CORES + core, here[one, :].T)
                    put(before * CORES + 1 - core, here[two, :].T)

        out = chain.call(
            "place_" + name,
            body,
            [*inputs, *old],
            [((unit, sz.width), f32)],
            alias={len(inputs): 0} if old else None,
        )
        state["out"] = out[0]

    def place_last(name):
        s = state[name]

        def body(done, step, old, rows, out_ref, step_ref, sems):
            chip, core = place()
            vector_copy = pltpu.make_async_copy(step, step_ref, sems.at[1])
            vector_copy.start()
            for h in range(CORES):
                cols = pl.ds(pl.multiple_of((chip * CORES + (core ^ h)) * unit, unit), unit)
                rows[:, cols] = done[h * unit : (h + 1) * unit, :].T
            rows_copy = pltpu.make_async_copy(rows, out_ref, sems.at[0])
            rows_copy.start()
            vector_copy.wait()
            rows_copy.wait()

        _, state["out"], state["step"] = chain.call(
            "place_" + name,
            body,
            [s["done"][0], state["step"], state["out"]],
            [((unit, sz.width), f32), ((unit, sz.width), f32), ((extra, LANES), f32)],
            outs=[VMEM, HBM, HBM],
            alias={2: 0},
            scratch=[pltpu.SemaphoreType.DMA((2,))],
        )

    for what in ORDER:
        if what == "V":
            start_vector()
        elif what[0] == "K":
            start(what[1], (int(what[2]),) if what[2:] else (1, 0))
        elif what[0] == "f":
            fold(what[1])
        elif what[1] == "1":
            first_sum(what[0])
        elif what[1] == "4":
            finish(what[0])
        elif what[1] == "5":
            (place_last if what[0] == LAST else place_blocks)(what[0])
        else:
            next_sum(what[0], int(what[1]) - 1)
    return state["out"], state["step"].reshape(-1)


def coupled(slices, slice_mix, lengths):
    count = slices.shape[0]
    coupling = (slice_mix + slice_mix.T) * 0.5 * (1.0 - jnp.eye(count, dtype=jnp.float32))
    blocks = lengths.shape[1]
    position = lax.broadcasted_iota(jnp.int32, (blocks, slices.shape[1] // blocks), 1)
    used = (position < lengths[0][:, None]).reshape(-1).astype(jnp.float32)
    out = []
    for k in range(count):
        total = coupling[k, 0] * slices[0].astype(jnp.float32)
        for l in range(1, count):
            total = total + coupling[k, l] * slices[l].astype(jnp.float32)
        out.append(total)
    return (jnp.stack(out) * used[None, :, None]).astype(jnp.bfloat16)


def whole(slices, slice_mix, lengths, search_step):
    width = slices.shape[2]
    left = slices.reshape(-1, width)
    right = coupled(slices, slice_mix, lengths).reshape(-1, width)
    rows = lax.psum_scatter(
        lax.dot_general(left, right, DIMS0, preferred_element_type=jnp.float32), AXIS, scatter_dimension=0, tiled=True
    )
    applied = jnp.dot(right, search_step, preferred_element_type=jnp.float32)
    head = applied.astype(jnp.bfloat16)
    tail = (applied - head.astype(jnp.float32)).astype(jnp.bfloat16)
    share = lax.dot_general(left, head, DIMS0, preferred_element_type=jnp.float32)
    share = share + lax.dot_general(left, tail, DIMS0, preferred_element_type=jnp.float32)
    return rows, lax.psum(share, AXIS)


def solution(mesh):
    devices = mesh.shape[AXIS]

    def on_device(slices, slice_mix, lengths, search_step):
        if fits(devices, slices, lengths):
            return halved(Sizes(devices, slices, lengths), slices, slice_mix, lengths, search_step)
        return whole(slices, slice_mix, lengths, search_step)

    return jax.shard_map(
        on_device,
        mesh=mesh,
        in_specs=(
            P(None, ("groups", AXIS), None),
            P(),
            P(("groups", AXIS), None),
            P("groups"),
        ),
        out_specs=(P(("groups", AXIS), None), P("groups")),
        check_vma=False,
    )
```

```python
import functools

import jax
import jax.numpy as jnp
from jax import lax
from jax.experimental import pallas as pl
from jax.experimental.pallas import tpu as pltpu
from jax.sharding import PartitionSpec as P

AXIS = "block"
CORES = 2
TILE = 16
LANES = 128
DIMS0 = (((0,), (0,)), ((), ()))
DIMS1 = (((1,), (1,)), ((), ()))
VMEM = pl.BlockSpec(memory_space=pltpu.VMEM)
HBM = pl.BlockSpec(memory_space=pltpu.HBM)
ANY = pl.BlockSpec(memory_space=pl.ANY)

PIECES = {
    "a": ((0,), (1, 2, 4)),
    "b": ((2,), (2, 4, 1)),
    "c": ((3,), (1, 2, 4)),
    "d": ((1, 4), (1, 2, 4)),
}
SPLIT = "abcd"
SWAPPERS = "bcd"
LAST = "a"
CARRIER = "c"
ORDER = (
    *("Kd1", "Kb1", "Ka1", "d1", "Kd0", "a1", "b1", "Kb0", "Ka0", "Kc1", "fb", "fa", "V", "fd"),
    *("Kc0", "c1", "d2", "b2", "fc", "d3", "c2", "b3", "a2", "c3", "d4", "b4", "a3", "c4"),
    *("d5", "b5", "c5", "a4", "a5"),
)


class Sizes:
    def __init__(self, devices, slices, lengths):
        self.devices = devices
        self.chips = devices // CORES
        self.count, self.rows, self.width = slices.shape
        self.blocks = lengths.shape[1]
        self.unit = self.width // devices
        self.step = self.rows // self.blocks
        most = self.step // TILE + ((self.blocks - 2) * self.step + (self.blocks - 1) * (TILE - 1)) // TILE
        self.chunk = 256 // self.count
        self.chunks = -(-most * TILE // self.chunk)
        self.tiles = self.chunks * self.chunk // TILE
        self.depth = self.count * self.chunks * self.chunk
        self.extended = self.width + 2 * CORES * self.unit

    def parts(self, shift):
        return 1 if 2 * shift == self.chips else CORES

    def piece_blocks(self, shifts):
        return sum(self.parts(k) for k in shifts)


def fits(devices, slices, lengths):
    unit, step = slices.shape[2] // devices, slices.shape[1] // lengths.shape[1]
    return devices == 16 and unit == LANES and slices.shape[0] == 4 and step % TILE == 0


def place():
    me = lax.axis_index(AXIS)
    return me // CORES, lax.rem(me, CORES)


def load_and_mix(sz, mix_hbm, lengths_hbm, slices_hbm, left_ref, right_ref, raw, mix_ref, lengths_ref, table, sems):
    first = pltpu.make_async_copy(lengths_hbm, lengths_ref, sems.at[sz.chunks])
    second = pltpu.make_async_copy(mix_hbm, mix_ref, sems.at[sz.chunks + 1])
    first.start()
    second.start()
    first.wait()
    for p in range(sz.tiles + 1):
        table[0, p] = 0
        table[1, p] = 0
    at = jnp.int32(0)
    for j in range(sz.blocks):
        for i in range(sz.step // TILE):
            inside = lengths_ref[0, j] - i * TILE
            at_safe = jnp.minimum(at, sz.tiles)
            table[0, at_safe] = jnp.where(inside > 0, j * sz.step + i * TILE, 0)
            table[1, at_safe] = jnp.clip(inside, 0, TILE)
            at = at + (inside > 0).astype(jnp.int32)
    per = sz.chunk // TILE
    for p in range(sz.tiles):
        source = pl.multiple_of(table[0, p], TILE)
        pltpu.make_async_copy(
            slices_hbm.at[:, pl.ds(source, TILE), :], raw.at[:, pl.ds(p * TILE, TILE), :], sems.at[p // per]
        ).start()
    second.wait()
    weight = {}
    for k in range(sz.count):
        for l in range(sz.count):
            if l != k:
                weight[k, l] = (mix_ref[k, l] + mix_ref[l, k]) * 0.5
    unit, wide = sz.unit, CORES * sz.unit
    _, core = place()

    def one_chunk(g, carry):
        here = pl.ds(pl.multiple_of(g * sz.chunk, sz.chunk), sz.chunk)
        pltpu.make_async_copy(slices_hbm.at[:, pl.ds(0, sz.chunk), :], raw.at[:, here, :], sems.at[g]).wait()
        base = g * sz.count * sz.chunk
        row = lax.broadcasted_iota(jnp.int32, (TILE, unit), 0)
        used = [row < table[1, g * per + p] for p in range(per)]

        def one_chip(i, carry):
            for c in range(CORES):
                cols = pl.ds(pl.multiple_of(i * wide + c * unit, unit), unit)
                mine = pl.ds(pl.multiple_of(i * wide + (c ^ core) * unit, unit), unit)
                block = raw[:, here, cols]
                turned = block.reshape(sz.count * sz.chunk, unit).T
                for p in range(per):
                    f = [block[k, p * TILE : (p + 1) * TILE].astype(jnp.float32) for k in range(sz.count)]
                    for k in range(sz.count):
                        total = None
                        for l in range(sz.count):
                            if l != k:
                                term = weight[k, l] * f[l]
                                total = term if total is None else total + term
                        to = pl.ds(pl.multiple_of(base + k * sz.chunk + p * TILE, TILE), TILE)
                        right_ref[to, mine] = jnp.where(used[p], total, 0.0).astype(jnp.bfloat16)
                left_ref[mine, pl.ds(pl.multiple_of(base, LANES), sz.count * sz.chunk)] = turned
            return carry

        lax.fori_loop(0, sz.chips, one_chip, 0, unroll=4)
        rows = pl.ds(pl.multiple_of(base, LANES), sz.count * sz.chunk)
        right_ref[rows, sz.width :] = right_ref[rows, : sz.extended - sz.width]
        return carry

    lax.fori_loop(0, sz.chunks, one_chunk, 0)


def runs(shifts):
    out = []
    for k in shifts:
        if out and out[-1][-1] + 1 == k:
            out[-1].append(k)
        else:
            out.append([k])
    return out


def multiply(sz, piece, bit, left_ref, right_ref, other_ref, own_ref, first=0):
    shifts, order = piece
    unit, chips = sz.unit, sz.chips
    blocks = sz.piece_blocks(shifts)
    wide = CORES * unit
    chip, _ = place()
    half = chips // 2
    for index in range(half):
        slot = bit * order[0]
        for n, mask in enumerate(order[1:]):
            slot += mask * ((index >> (len(order) - 2 - n)) & 1)
        row = chip ^ slot
        at = first // unit + index * blocks
        for run in runs(shifts):
            col = lax.rem(row + run[0], chips)
            tile = jnp.dot(
                left_ref[pl.ds(pl.multiple_of(row * wide, wide), wide), :],
                right_ref[:, pl.ds(pl.multiple_of(col * wide, wide), wide * len(run))],
                preferred_element_type=jnp.float32,
            )
            for n, k in enumerate(run):
                for ref, owner in ((own_ref, 0), (other_ref, 1)):
                    if 2 * k == chips:
                        rows = tile[owner * unit : (owner + 1) * unit, n * wide : (n + 1) * wide]
                        same, cross = (rows[:, (owner ^ f) * unit : ((owner ^ f) + 1) * unit] for f in (0, 1))
                        ref[at * unit : (at + 1) * unit, :] = jnp.where(row >= half, cross, same)
                    else:
                        left = n * wide + owner * unit
                        for h in range(CORES):
                            rows = owner ^ h
                            ref[(at + h) * unit : (at + h + 1) * unit, :] = tile[
                                rows * unit : (rows + 1) * unit, left : left + unit
                            ]
                at += sz.parts(k)


def vector(sz, left_ref, right_ref, step_ref, outs):
    unit = sz.unit
    _, core = place()
    turned = []
    for d in range(sz.devices):
        turned.append(step_ref[:, pl.ds(pl.multiple_of((d ^ core) * unit, unit), unit)])
    x = jnp.broadcast_to(jnp.concatenate(turned, axis=1), (8, sz.width))
    applied = lax.dot_general(x, right_ref[:, : sz.width], DIMS1, preferred_element_type=jnp.float32)
    head = applied.astype(jnp.bfloat16).astype(jnp.float32)
    row = lax.broadcasted_iota(jnp.int32, applied.shape, 0)
    both = jnp.where(row == 0, head, jnp.where(row == 1, applied - head, 0.0)).astype(jnp.bfloat16)
    share = lax.dot_general(both, left_ref[...], DIMS1, preferred_element_type=jnp.float32)
    share = share[0:1, :] + share[1:2, :]
    for ref in outs:
        first = ref.shape[0] - sz.devices
        for d in range(sz.devices):
            ref[pl.ds(first + (d ^ core), 1), :] = share[:, d * unit : (d + 1) * unit]


def add_rows(to, at, size, *terms):
    block = LANES if size % LANES == 0 else size

    def one(i, carry):
        total = None
        for ref, first in terms:
            value = ref[pl.ds(pl.multiple_of(first + i * block, 8), block), :]
            total = value if total is None else total + value
        to[pl.ds(pl.multiple_of(at + i * block, 8), block), :] = total
        return carry

    lax.fori_loop(0, size // block, one, 0)


class Chain:
    def __init__(self):
        self.token = None

    def call(self, name, body, inputs, shapes, scratch=(), specs=None, outs=None, alias=None, flops=0, vmem=4):
        specs = list(specs or [VMEM] * len(inputs))
        inputs = list(inputs)
        count = len(inputs)
        if self.token is not None:
            inputs.append(self.token)
            specs.append(ANY)

        def kernel(*refs):
            body(*refs[:count], *refs[len(inputs) :])

        out = pl.pallas_call(
            kernel,
            in_specs=specs,
            out_specs=outs or [VMEM] * len(shapes),
            input_output_aliases=alias or {},
            out_shape=[jax.ShapeDtypeStruct(s, d) for s, d in shapes],
            scratch_shapes=list(scratch),
            cost_estimate=pl.CostEstimate(flops=flops, bytes_accessed=0, transcendentals=0),
            compiler_params=pltpu.CompilerParams(vmem_limit_bytes=vmem << 20),
            name=name,
        )(*inputs)
        self.token = out[0]
        return out


def send(x, chips, to):
    pairs = []
    for chip in range(chips):
        for core in range(CORES):
            other, its_core = to(chip, core)
            pairs.append((chip * CORES + core, other * CORES + its_core))
    return lax.ppermute(x, AXIS, pairs)


def to_core(x, chips):
    return send(x, chips, lambda m, c: (m, 1 - c))


def across(x, chips, mask):
    return send(x, chips, lambda m, c: (m ^ mask, c))


def mirror(x, chips, shift):
    def to(m, c):
        flip = int(m >= shift) if 2 * shift == chips else 0
        return (m + shift) % chips, c ^ flip

    return send(x, chips, to)


def halved(sz, slices, slice_mix, lengths, search_step):
    chips, unit, f32 = sz.chips, sz.unit, jnp.float32
    chain = Chain()
    extra = sz.width // LANES
    state = {"swaps": []}
    step_row = search_step.reshape(1, -1)

    def tail(name):
        return extra if name == CARRIER else 0

    def start(name, bits):
        piece = PIECES[name]
        shifts = piece[0]
        half = chips // 2 * sz.piece_blocks(shifts) * unit
        rows = half * len(bits)
        shapes = [((rows, LANES), f32)] * 2
        flops = chips * (CORES * unit) ** 2 * len(shifts) * sz.depth * len(bits)
        if "left" not in state:

            def body(mix_hbm, lengths_hbm, slices_hbm, left_ref, right_ref, other_ref, own_ref, *scratch):
                load_and_mix(sz, mix_hbm, lengths_hbm, slices_hbm, left_ref, right_ref, *scratch)
                multiply(sz, piece, bits[0], left_ref, right_ref, other_ref, own_ref)

            out = chain.call(
                "first",
                body,
                [pltpu.with_memory_space_constraint(a, pltpu.HBM) for a in (slice_mix, lengths, slices)],
                [((sz.width, sz.depth), jnp.bfloat16), ((sz.depth, sz.extended), jnp.bfloat16)] + shapes,
                scratch=[
                    pltpu.VMEM((sz.count, sz.chunks * sz.chunk, sz.width), jnp.bfloat16),
                    pltpu.SMEM(slice_mix.shape, f32),
                    pltpu.SMEM(lengths.shape, jnp.int32),
                    pltpu.SMEM((2, sz.tiles + 1), jnp.int32),
                    pltpu.SemaphoreType.DMA((sz.chunks + 2,)),
                ],
                specs=[HBM] * 3,
                flops=flops,
                vmem=12,
            )
            state["left"], state["right"] = out[:2]
            other, own = out[2:]
        else:

            def body(left_ref, right_ref, other_ref, own_ref):
                for n, bit in enumerate(bits):
                    multiply(sz, piece, bit, left_ref, right_ref, other_ref, own_ref, n * half)

            other, own = chain.call(
                "multiply_" + name,
                body,
                [state["left"], state["right"]],
                shapes,
                flops=flops,
                vmem=8,
            )
        s = state.setdefault(name, {})
        n = bits[0] if len(bits) == 1 else ""
        s[f"own{n}"], s[f"came{n}"] = own, to_core(other, chips)

    def start_vector():
        def body(left_ref, right_ref, step_ref, out_ref):
            vector(sz, left_ref, right_ref, step_ref, [out_ref])

        share = chain.call(
            "vector", body, [state["left"], state["right"], step_row], [((extra, LANES), f32)], vmem=8
        )[0]
        state["vector"] = [share, to_core(share, chips)]

    def first_sum(name):
        s = state[name]
        half = chips // 2 * sz.piece_blocks(PIECES[name][0]) * unit
        more = tail(name)
        if name in SPLIT:

            def body(own, came, *refs):
                add_rows(refs[-1], 0, half, (own, 0), (came, 0))
                if more:
                    add_rows(refs[-1], half, more, (refs[0], 0), (refs[1], 0))

            inputs = [s["own1"], s["came1"], *(state["vector"] if more else [])]
            s["sent"] = chain.call("sum1_" + name, body, inputs, [((half + more, LANES), f32)])[0]
        else:

            def body(own, came, *refs):
                send_ref, keep_ref = refs[-2:]
                add_rows(send_ref, 0, half, (own, 0), (came, 0))
                add_rows(keep_ref, 0, half, (own, half), (came, half))
                if more:
                    add_rows(send_ref, half, more, (refs[0], 0), (refs[1], 0))

            s["sent"], s["kept"] = chain.call(
                "sum1_" + name,
                body,
                [s["own"], s["came"], *(state["vector"] if more else [])],
                [((half + more, LANES), f32), ((half, LANES), f32)],
            )
        s["came"] = across(s["sent"], chips, PIECES[name][1][0])

    def fold(name):
        s = state[name]
        rows = s["own0"].shape[0]

        def body(own, came, out):
            add_rows(out, 0, rows, (own, 0), (came, 0))

        s["kept"] = chain.call("fold_" + name, body, [s["own0"], s["came0"]], [((rows, LANES), f32)])[0]

    def next_sum(name, n):
        s = state[name]
        shifts, order = PIECES[name]
        full = s["kept"].shape[0]
        rows = full // 2
        more = tail(name)
        half = first_row(shifts, chips // 2) if n == len(order) - 1 and chips // 2 in shifts else None
        both = 0 if half is None else unit

        def body(kept, sent, came, send_ref, keep_ref):
            add_rows(send_ref, 0, rows, (kept, rows), (came, rows))
            add_rows(keep_ref, 0, rows, (kept, 0), (came, 0))
            if both:
                add_rows(send_ref, rows, both, (kept, half), (came, half))
            if more:
                add_rows(send_ref, rows + both, more, (sent, full), (came, full))

        s["sent"], s["kept"] = chain.call(
            f"sum{n + 1}_" + name,
            body,
            [s["kept"], s["sent"], s["came"]],
            [((rows + both + more, LANES), f32), ((rows, LANES), f32)],
        )
        s["came"] = across(s["sent"], chips, order[n])

    def first_row(shifts, shift):
        return unit * sz.piece_blocks([k for k in shifts if k < shift])

    def finish(name):
        s = state[name]
        shifts = PIECES[name][0]
        rows = s["kept"].shape[0]
        more = tail(name)
        swapped = [k for k in shifts if k]
        last = name in SWAPPERS
        before = list(state["swaps"]) if last else []
        shapes = [((CORES * unit, LANES), f32) for k in shifts]
        if last:
            shapes.append((((len(swapped) + len(before)) * unit, LANES), f32))
        if more:
            shapes.append(((extra, LANES), f32))

        def body(kept, sent, came, *refs):
            outs = refs[len(before) :]
            for n, k in enumerate(shifts):
                at = first_row(shifts, k)
                terms = [((kept, at + h * unit), (came, at + h * unit)) for h in range(sz.parts(k))]
                if 2 * k == chips:
                    terms.append(((sent, at), (came, rows)))
                for h, pair in enumerate(terms):
                    add_rows(outs[n], h * unit, unit, *pair)
                if last and k in swapped:
                    add_rows(outs[len(shifts)], (len(before) + swapped.index(k)) * unit, unit, *terms[1])
            for n, (_, _, row, _) in enumerate(before):
                add_rows(outs[len(shifts)], n * unit, unit, (refs[n], row))
            if more:
                add_rows(outs[-1], 0, extra, (sent, rows), (came, rows))

        out = chain.call("done_" + name, body, [s["kept"], s["sent"], s["came"], *(b[0] for b in before)], shapes)
        s["done"] = list(out[: len(shifts)])
        s["plan"] = [(k, "own", n, 0) for n, k in enumerate(shifts)]
        for k in swapped:
            if 2 * k != chips:
                s["plan"].append((k, "mirrored", len(s["done"]), 0))
                s["done"].append(mirror(out[shifts.index(k)], chips, k))
        for n, k in enumerate(swapped):
            state["swaps"].append((out[shifts.index(k)], k, unit, name))
        if last:
            for n, (_, k, _, _) in enumerate(state["swaps"]):
                s["plan"].append((k, "swapped", len(s["done"]), n * unit))
            s["done"].append(to_core(out[len(shifts)], chips))
            state["swaps"] = []
        if more:
            state["step"] = out[-1]

    def place_blocks(name):
        s = state[name]
        inputs, plan = s["done"], s["plan"]
        old = [state["out"]] if "out" in state else []

        def body(*refs):
            chip, core = place()
            to = refs[len(inputs) + len(old)]

            def put(device, value):
                to[:, pl.ds(pl.multiple_of(device * unit, unit), unit)] = value

            for k, kind, n, first in plan:
                here = refs[n]
                after, before = lax.rem(chip + k, chips), lax.rem(chip + chips - k, chips)
                one, two = (slice(first + h * unit, first + (h + 1) * unit) for h in range(2))
                low = (chip >= k).astype(jnp.int32)
                if 2 * k == chips and kind == "own":
                    put(after * CORES + (core ^ low), here[one, :])
                    mine = (here, two)
                elif 2 * k == chips:
                    value = jnp.where(low > 0, mine[0][mine[1], :], here[one, :])
                    put(after * CORES + (core ^ (1 - low)), value.T)
                elif kind == "own":
                    put(after * CORES + core, here[one, :])
                elif kind == "swapped":
                    put(after * CORES + 1 - core, here[one, :])
                else:
                    put(before * CORES + core, here[one, :].T)
                    put(before * CORES + 1 - core, here[two, :].T)

        out = chain.call(
            "place_" + name,
            body,
            [*inputs, *old],
            [((unit, sz.width), f32)],
            alias={len(inputs): 0} if old else None,
        )
        state["out"] = out[0]

    def place_last(name):
        s = state[name]

        def body(done, step, old, rows, out_ref, step_ref, sems):
            chip, core = place()
            vector_copy = pltpu.make_async_copy(step, step_ref, sems.at[1])
            vector_copy.start()
            for h in range(CORES):
                cols = pl.ds(pl.multiple_of((chip * CORES + (core ^ h)) * unit, unit), unit)
                rows[:, cols] = done[h * unit : (h + 1) * unit, :].T
            rows_copy = pltpu.make_async_copy(rows, out_ref, sems.at[0])
            rows_copy.start()
            vector_copy.wait()
            rows_copy.wait()

        _, state["out"], state["step"] = chain.call(
            "place_" + name,
            body,
            [s["done"][0], state["step"], state["out"]],
            [((unit, sz.width), f32), ((unit, sz.width), f32), ((extra, LANES), f32)],
            outs=[VMEM, HBM, HBM],
            alias={2: 0},
            scratch=[pltpu.SemaphoreType.DMA((2,))],
        )

    for what in ORDER:
        if what == "V":
            start_vector()
        elif what[0] == "K":
            start(what[1], (int(what[2]),) if what[2:] else (1, 0))
        elif what[0] == "f":
            fold(what[1])
        elif what[1] == "1":
            first_sum(what[0])
        elif what[1] == "4":
            finish(what[0])
        elif what[1] == "5":
            (place_last if what[0] == LAST else place_blocks)(what[0])
        else:
            next_sum(what[0], int(what[1]) - 1)
    return state["out"], state["step"].reshape(-1)


def coupled(slices, slice_mix, lengths):
    count = slices.shape[0]
    coupling = (slice_mix + slice_mix.T) * 0.5 * (1.0 - jnp.eye(count, dtype=jnp.float32))
    blocks = lengths.shape[1]
    position = lax.broadcasted_iota(jnp.int32, (blocks, slices.shape[1] // blocks), 1)
    used = (position < lengths[0][:, None]).reshape(-1).astype(jnp.float32)
    out = []
    for k in range(count):
        total = coupling[k, 0] * slices[0].astype(jnp.float32)
        for l in range(1, count):
            total = total + coupling[k, l] * slices[l].astype(jnp.float32)
        out.append(total)
    return (jnp.stack(out) * used[None, :, None]).astype(jnp.bfloat16)


def whole(slices, slice_mix, lengths, search_step):
    width = slices.shape[2]
    left = slices.reshape(-1, width)
    right = coupled(slices, slice_mix, lengths).reshape(-1, width)
    rows = lax.psum_scatter(
        lax.dot_general(left, right, DIMS0, preferred_element_type=jnp.float32), AXIS, scatter_dimension=0, tiled=True
    )
    applied = jnp.dot(right, search_step, preferred_element_type=jnp.float32)
    head = applied.astype(jnp.bfloat16)
    tail = (applied - head.astype(jnp.float32)).astype(jnp.bfloat16)
    share = lax.dot_general(left, head, DIMS0, preferred_element_type=jnp.float32)
    share = share + lax.dot_general(left, tail, DIMS0, preferred_element_type=jnp.float32)
    return rows, lax.psum(share, AXIS)


def solution(mesh):
    devices = mesh.shape[AXIS]

    def on_device(slices, slice_mix, lengths, search_step):
        if fits(devices, slices, lengths):
            return halved(Sizes(devices, slices, lengths), slices, slice_mix, lengths, search_step)
        return whole(slices, slice_mix, lengths, search_step)

    return jax.shard_map(
        on_device,
        mesh=mesh,
        in_specs=(
            P(None, ("groups", AXIS), None),
            P(),
            P(("groups", AXIS), None),
            P("groups"),
        ),
        out_specs=(P(("groups", AXIS), None), P("groups")),
        check_vma=False,
    )
```

```python
import functools

import jax
import jax.numpy as jnp
from jax import lax
from jax.experimental import pallas as pl
from jax.experimental.pallas import tpu as pltpu
from jax.sharding import PartitionSpec as P

AXIS = "block"
CORES = 2
TILE = 16
LANES = 128
DIMS0 = (((0,), (0,)), ((), ()))
DIMS1 = (((1,), (1,)), ((), ()))
VMEM = pl.BlockSpec(memory_space=pltpu.VMEM)
HBM = pl.BlockSpec(memory_space=pltpu.HBM)
ANY = pl.BlockSpec(memory_space=pl.ANY)

PIECES = {
    "a": ((0,), (1, 2, 4)),
    "b": ((2,), (2, 4, 1)),
    "c": ((3,), (1, 2, 4)),
    "d": ((1, 4), (1, 2, 4)),
}
SPLIT = "abcd"
SWAPPERS = "bcd"
LAST = "a"
CARRIER = "b"
ORDER = (
    *("Kd1", "Kd0", "Kb1", "d1", "Kb0", "Ka1", "V", "Kc0", "fb", "b1", "fd", "Kc1", "c1", "Ka0"),
    *("a1", "fc", "d2", "b2", "c2", "d3", "fa", "b3", "a2", "c3", "d4", "b4", "a3", "c4"),
    *("b5", "c5", "d5", "a4", "a5"),
)


class Sizes:
    def __init__(self, devices, slices, lengths):
        self.devices = devices
        self.chips = devices // CORES
        self.count, self.rows, self.width = slices.shape
        self.blocks = lengths.shape[1]
        self.unit = self.width // devices
        self.step = self.rows // self.blocks
        most = self.step // TILE + ((self.blocks - 2) * self.step + (self.blocks - 1) * (TILE - 1)) // TILE
        self.chunk = 256 // self.count
        self.chunks = -(-most * TILE // self.chunk)
        self.tiles = self.chunks * self.chunk // TILE
        self.depth = self.count * self.chunks * self.chunk
        self.extended = self.width + 2 * CORES * self.unit

    def parts(self, shift):
        return 1 if 2 * shift == self.chips else CORES

    def piece_blocks(self, shifts):
        return sum(self.parts(k) for k in shifts)


def fits(devices, slices, lengths):
    unit, step = slices.shape[2] // devices, slices.shape[1] // lengths.shape[1]
    return devices == 16 and unit == LANES and slices.shape[0] == 4 and step % TILE == 0


def place():
    me = lax.axis_index(AXIS)
    return me // CORES, lax.rem(me, CORES)


def load_and_mix(sz, mix_hbm, lengths_hbm, slices_hbm, left_ref, right_ref, raw, mix_ref, lengths_ref, table, sems):
    first = pltpu.make_async_copy(lengths_hbm, lengths_ref, sems.at[sz.chunks])
    second = pltpu.make_async_copy(mix_hbm, mix_ref, sems.at[sz.chunks + 1])
    first.start()
    second.start()
    first.wait()
    for p in range(sz.tiles + 1):
        table[0, p] = 0
        table[1, p] = 0
    at = jnp.int32(0)
    for j in range(sz.blocks):
        for i in range(sz.step // TILE):
            inside = lengths_ref[0, j] - i * TILE
            at_safe = jnp.minimum(at, sz.tiles)
            table[0, at_safe] = jnp.where(inside > 0, j * sz.step + i * TILE, 0)
            table[1, at_safe] = jnp.clip(inside, 0, TILE)
            at = at + (inside > 0).astype(jnp.int32)
    per = sz.chunk // TILE
    for p in range(sz.tiles):
        source = pl.multiple_of(table[0, p], TILE)
        pltpu.make_async_copy(
            slices_hbm.at[:, pl.ds(source, TILE), :], raw.at[:, pl.ds(p * TILE, TILE), :], sems.at[p // per]
        ).start()
    second.wait()
    weight = {}
    for k in range(sz.count):
        for l in range(sz.count):
            if l != k:
                weight[k, l] = (mix_ref[k, l] + mix_ref[l, k]) * 0.5
    unit, wide = sz.unit, CORES * sz.unit
    _, core = place()

    def one_chunk(g, carry):
        here = pl.ds(pl.multiple_of(g * sz.chunk, sz.chunk), sz.chunk)
        pltpu.make_async_copy(slices_hbm.at[:, pl.ds(0, sz.chunk), :], raw.at[:, here, :], sems.at[g]).wait()
        base = g * sz.count * sz.chunk
        row = lax.broadcasted_iota(jnp.int32, (TILE, unit), 0)
        used = [row < table[1, g * per + p] for p in range(per)]

        def one_chip(i, carry):
            for c in range(CORES):
                cols = pl.ds(pl.multiple_of(i * wide + c * unit, unit), unit)
                mine = pl.ds(pl.multiple_of(i * wide + (c ^ core) * unit, unit), unit)
                block = raw[:, here, cols]
                turned = block.reshape(sz.count * sz.chunk, unit).T
                for p in range(per):
                    f = [block[k, p * TILE : (p + 1) * TILE].astype(jnp.float32) for k in range(sz.count)]
                    for k in range(sz.count):
                        total = None
                        for l in range(sz.count):
                            if l != k:
                                term = weight[k, l] * f[l]
                                total = term if total is None else total + term
                        to = pl.ds(pl.multiple_of(base + k * sz.chunk + p * TILE, TILE), TILE)
                        right_ref[to, mine] = jnp.where(used[p], total, 0.0).astype(jnp.bfloat16)
                left_ref[mine, pl.ds(pl.multiple_of(base, LANES), sz.count * sz.chunk)] = turned
            return carry

        lax.fori_loop(0, sz.chips, one_chip, 0, unroll=4)
        rows = pl.ds(pl.multiple_of(base, LANES), sz.count * sz.chunk)
        right_ref[rows, sz.width :] = right_ref[rows, : sz.extended - sz.width]
        return carry

    lax.fori_loop(0, sz.chunks, one_chunk, 0)


def runs(shifts):
    out = []
    for k in shifts:
        if out and out[-1][-1] + 1 == k:
            out[-1].append(k)
        else:
            out.append([k])
    return out


def multiply(sz, piece, bit, left_ref, right_ref, other_ref, own_ref, first=0):
    shifts, order = piece
    unit, chips = sz.unit, sz.chips
    blocks = sz.piece_blocks(shifts)
    wide = CORES * unit
    chip, _ = place()
    half = chips // 2
    for index in range(half):
        slot = bit * order[0]
        for n, mask in enumerate(order[1:]):
            slot += mask * ((index >> (len(order) - 2 - n)) & 1)
        row = chip ^ slot
        at = first // unit + index * blocks
        for run in runs(shifts):
            col = lax.rem(row + run[0], chips)
            tile = jnp.dot(
                left_ref[pl.ds(pl.multiple_of(row * wide, wide), wide), :],
                right_ref[:, pl.ds(pl.multiple_of(col * wide, wide), wide * len(run))],
                preferred_element_type=jnp.float32,
            )
            for n, k in enumerate(run):
                for ref, owner in ((own_ref, 0), (other_ref, 1)):
                    if 2 * k == chips:
                        rows = tile[owner * unit : (owner + 1) * unit, n * wide : (n + 1) * wide]
                        same, cross = (rows[:, (owner ^ f) * unit : ((owner ^ f) + 1) * unit] for f in (0, 1))
                        ref[at * unit : (at + 1) * unit, :] = jnp.where(row >= half, cross, same)
                    else:
                        left = n * wide + owner * unit
                        for h in range(CORES):
                            rows = owner ^ h
                            ref[(at + h) * unit : (at + h + 1) * unit, :] = tile[
                                rows * unit : (rows + 1) * unit, left : left + unit
                            ]
                at += sz.parts(k)


def vector(sz, left_ref, right_ref, step_ref, outs):
    unit = sz.unit
    _, core = place()
    turned = []
    for d in range(sz.devices):
        turned.append(step_ref[:, pl.ds(pl.multiple_of((d ^ core) * unit, unit), unit)])
    x = jnp.broadcast_to(jnp.concatenate(turned, axis=1), (8, sz.width))
    applied = lax.dot_general(x, right_ref[:, : sz.width], DIMS1, preferred_element_type=jnp.float32)
    head = applied.astype(jnp.bfloat16).astype(jnp.float32)
    row = lax.broadcasted_iota(jnp.int32, applied.shape, 0)
    both = jnp.where(row == 0, head, jnp.where(row == 1, applied - head, 0.0)).astype(jnp.bfloat16)
    share = lax.dot_general(both, left_ref[...], DIMS1, preferred_element_type=jnp.float32)
    share = share[0:1, :] + share[1:2, :]
    for ref in outs:
        first = ref.shape[0] - sz.devices
        for d in range(sz.devices):
            ref[pl.ds(first + (d ^ core), 1), :] = share[:, d * unit : (d + 1) * unit]


def add_rows(to, at, size, *terms):
    block = LANES if size % LANES == 0 else size

    def one(i, carry):
        total = None
        for ref, first in terms:
            value = ref[pl.ds(pl.multiple_of(first + i * block, 8), block), :]
            total = value if total is None else total + value
        to[pl.ds(pl.multiple_of(at + i * block, 8), block), :] = total
        return carry

    lax.fori_loop(0, size // block, one, 0)


class Chain:
    def __init__(self):
        self.token = None

    def call(self, name, body, inputs, shapes, scratch=(), specs=None, outs=None, alias=None, flops=0, vmem=4):
        specs = list(specs or [VMEM] * len(inputs))
        inputs = list(inputs)
        count = len(inputs)
        if self.token is not None:
            inputs.append(self.token)
            specs.append(ANY)

        def kernel(*refs):
            body(*refs[:count], *refs[len(inputs) :])

        out = pl.pallas_call(
            kernel,
            in_specs=specs,
            out_specs=outs or [VMEM] * len(shapes),
            input_output_aliases=alias or {},
            out_shape=[jax.ShapeDtypeStruct(s, d) for s, d in shapes],
            scratch_shapes=list(scratch),
            cost_estimate=pl.CostEstimate(flops=flops, bytes_accessed=0, transcendentals=0),
            compiler_params=pltpu.CompilerParams(vmem_limit_bytes=vmem << 20),
            name=name,
        )(*inputs)
        self.token = out[0]
        return out


def send(x, chips, to):
    pairs = []
    for chip in range(chips):
        for core in range(CORES):
            other, its_core = to(chip, core)
            pairs.append((chip * CORES + core, other * CORES + its_core))
    return lax.ppermute(x, AXIS, pairs)


def to_core(x, chips):
    return send(x, chips, lambda m, c: (m, 1 - c))


def across(x, chips, mask):
    return send(x, chips, lambda m, c: (m ^ mask, c))


def mirror(x, chips, shift):
    def to(m, c):
        flip = int(m >= shift) if 2 * shift == chips else 0
        return (m + shift) % chips, c ^ flip

    return send(x, chips, to)


def halved(sz, slices, slice_mix, lengths, search_step):
    chips, unit, f32 = sz.chips, sz.unit, jnp.float32
    chain = Chain()
    extra = sz.width // LANES
    state = {"swaps": []}
    step_row = search_step.reshape(1, -1)

    def tail(name):
        return extra if name == CARRIER else 0

    def start(name, bits):
        piece = PIECES[name]
        shifts = piece[0]
        half = chips // 2 * sz.piece_blocks(shifts) * unit
        rows = half * len(bits)
        shapes = [((rows, LANES), f32)] * 2
        flops = chips * (CORES * unit) ** 2 * len(shifts) * sz.depth * len(bits)
        if "left" not in state:

            def body(mix_hbm, lengths_hbm, slices_hbm, left_ref, right_ref, other_ref, own_ref, *scratch):
                load_and_mix(sz, mix_hbm, lengths_hbm, slices_hbm, left_ref, right_ref, *scratch)
                multiply(sz, piece, bits[0], left_ref, right_ref, other_ref, own_ref)

            out = chain.call(
                "first",
                body,
                [pltpu.with_memory_space_constraint(a, pltpu.HBM) for a in (slice_mix, lengths, slices)],
                [((sz.width, sz.depth), jnp.bfloat16), ((sz.depth, sz.extended), jnp.bfloat16)] + shapes,
                scratch=[
                    pltpu.VMEM((sz.count, sz.chunks * sz.chunk, sz.width), jnp.bfloat16),
                    pltpu.SMEM(slice_mix.shape, f32),
                    pltpu.SMEM(lengths.shape, jnp.int32),
                    pltpu.SMEM((2, sz.tiles + 1), jnp.int32),
                    pltpu.SemaphoreType.DMA((sz.chunks + 2,)),
                ],
                specs=[HBM] * 3,
                flops=flops,
                vmem=12,
            )
            state["left"], state["right"] = out[:2]
            other, own = out[2:]
        else:

            def body(left_ref, right_ref, other_ref, own_ref):
                for n, bit in enumerate(bits):
                    multiply(sz, piece, bit, left_ref, right_ref, other_ref, own_ref, n * half)

            other, own = chain.call(
                "multiply_" + name,
                body,
                [state["left"], state["right"]],
                shapes,
                flops=flops,
                vmem=8,
            )
        s = state.setdefault(name, {})
        n = bits[0] if len(bits) == 1 else ""
        s[f"own{n}"], s[f"came{n}"] = own, to_core(other, chips)

    def start_vector():
        def body(left_ref, right_ref, step_ref, out_ref):
            vector(sz, left_ref, right_ref, step_ref, [out_ref])

        share = chain.call(
            "vector", body, [state["left"], state["right"], step_row], [((extra, LANES), f32)], vmem=8
        )[0]
        state["vector"] = [share, to_core(share, chips)]

    def first_sum(name):
        s = state[name]
        half = chips // 2 * sz.piece_blocks(PIECES[name][0]) * unit
        more = tail(name)
        if name in SPLIT:

            def body(own, came, *refs):
                add_rows(refs[-1], 0, half, (own, 0), (came, 0))
                if more:
                    add_rows(refs[-1], half, more, (refs[0], 0), (refs[1], 0))

            inputs = [s["own1"], s["came1"], *(state["vector"] if more else [])]
            s["sent"] = chain.call("sum1_" + name, body, inputs, [((half + more, LANES), f32)])[0]
        else:

            def body(own, came, *refs):
                send_ref, keep_ref = refs[-2:]
                add_rows(send_ref, 0, half, (own, 0), (came, 0))
                add_rows(keep_ref, 0, half, (own, half), (came, half))
                if more:
                    add_rows(send_ref, half, more, (refs[0], 0), (refs[1], 0))

            s["sent"], s["kept"] = chain.call(
                "sum1_" + name,
                body,
                [s["own"], s["came"], *(state["vector"] if more else [])],
                [((half + more, LANES), f32), ((half, LANES), f32)],
            )
        s["came"] = across(s["sent"], chips, PIECES[name][1][0])

    def fold(name):
        s = state[name]
        rows = s["own0"].shape[0]

        def body(own, came, out):
            add_rows(out, 0, rows, (own, 0), (came, 0))

        s["kept"] = chain.call("fold_" + name, body, [s["own0"], s["came0"]], [((rows, LANES), f32)])[0]

    def next_sum(name, n):
        s = state[name]
        shifts, order = PIECES[name]
        full = s["kept"].shape[0]
        rows = full // 2
        more = tail(name)
        half = first_row(shifts, chips // 2) if n == len(order) - 1 and chips // 2 in shifts else None
        both = 0 if half is None else unit

        def body(kept, sent, came, send_ref, keep_ref):
            add_rows(send_ref, 0, rows, (kept, rows), (came, rows))
            add_rows(keep_ref, 0, rows, (kept, 0), (came, 0))
            if both:
                add_rows(send_ref, rows, both, (kept, half), (came, half))
            if more:
                add_rows(send_ref, rows + both, more, (sent, full), (came, full))

        s["sent"], s["kept"] = chain.call(
            f"sum{n + 1}_" + name,
            body,
            [s["kept"], s["sent"], s["came"]],
            [((rows + both + more, LANES), f32), ((rows, LANES), f32)],
        )
        s["came"] = across(s["sent"], chips, order[n])

    def first_row(shifts, shift):
        return unit * sz.piece_blocks([k for k in shifts if k < shift])

    def finish(name):
        s = state[name]
        shifts = PIECES[name][0]
        rows = s["kept"].shape[0]
        more = tail(name)
        swapped = [k for k in shifts if k]
        last = name in SWAPPERS
        before = list(state["swaps"]) if last else []
        shapes = [((CORES * unit, LANES), f32) for k in shifts]
        if last:
            shapes.append((((len(swapped) + len(before)) * unit, LANES), f32))
        if more:
            shapes.append(((extra, LANES), f32))

        def body(kept, sent, came, *refs):
            outs = refs[len(before) :]
            for n, k in enumerate(shifts):
                at = first_row(shifts, k)
                terms = [((kept, at + h * unit), (came, at + h * unit)) for h in range(sz.parts(k))]
                if 2 * k == chips:
                    terms.append(((sent, at), (came, rows)))
                for h, pair in enumerate(terms):
                    add_rows(outs[n], h * unit, unit, *pair)
                if last and k in swapped:
                    add_rows(outs[len(shifts)], (len(before) + swapped.index(k)) * unit, unit, *terms[1])
            for n, (_, _, row, _) in enumerate(before):
                add_rows(outs[len(shifts)], n * unit, unit, (refs[n], row))
            if more:
                add_rows(outs[-1], 0, extra, (sent, rows), (came, rows))

        out = chain.call("done_" + name, body, [s["kept"], s["sent"], s["came"], *(b[0] for b in before)], shapes)
        s["done"] = list(out[: len(shifts)])
        s["plan"] = [(k, "own", n, 0) for n, k in enumerate(shifts)]
        for k in swapped:
            if 2 * k != chips:
                s["plan"].append((k, "mirrored", len(s["done"]), 0))
                s["done"].append(mirror(out[shifts.index(k)], chips, k))
        for n, k in enumerate(swapped):
            state["swaps"].append((out[shifts.index(k)], k, unit, name))
        if last:
            for n, (_, k, _, _) in enumerate(state["swaps"]):
                s["plan"].append((k, "swapped", len(s["done"]), n * unit))
            s["done"].append(to_core(out[len(shifts)], chips))
            state["swaps"] = []
        if more:
            state["step"] = out[-1]

    def place_blocks(name):
        s = state[name]
        inputs, plan = s["done"], s["plan"]
        old = [state["out"]] if "out" in state else []

        def body(*refs):
            chip, core = place()
            to = refs[len(inputs) + len(old)]

            def put(device, value):
                to[:, pl.ds(pl.multiple_of(device * unit, unit), unit)] = value

            for k, kind, n, first in plan:
                here = refs[n]
                after, before = lax.rem(chip + k, chips), lax.rem(chip + chips - k, chips)
                one, two = (slice(first + h * unit, first + (h + 1) * unit) for h in range(2))
                low = (chip >= k).astype(jnp.int32)
                if 2 * k == chips and kind == "own":
                    put(after * CORES + (core ^ low), here[one, :])
                    mine = (here, two)
                elif 2 * k == chips:
                    value = jnp.where(low > 0, mine[0][mine[1], :], here[one, :])
                    put(after * CORES + (core ^ (1 - low)), value.T)
                elif kind == "own":
                    put(after * CORES + core, here[one, :])
                elif kind == "swapped":
                    put(after * CORES + 1 - core, here[one, :])
                else:
                    put(before * CORES + core, here[one, :].T)
                    put(before * CORES + 1 - core, here[two, :].T)

        out = chain.call(
            "place_" + name,
            body,
            [*inputs, *old],
            [((unit, sz.width), f32)],
            alias={len(inputs): 0} if old else None,
        )
        state["out"] = out[0]

    def place_last(name):
        s = state[name]

        def body(done, step, old, rows, out_ref, step_ref, sems):
            chip, core = place()
            vector_copy = pltpu.make_async_copy(step, step_ref, sems.at[1])
            vector_copy.start()
            for h in range(CORES):
                cols = pl.ds(pl.multiple_of((chip * CORES + (core ^ h)) * unit, unit), unit)
                rows[:, cols] = done[h * unit : (h + 1) * unit, :].T
            rows_copy = pltpu.make_async_copy(rows, out_ref, sems.at[0])
            rows_copy.start()
            vector_copy.wait()
            rows_copy.wait()

        _, state["out"], state["step"] = chain.call(
            "place_" + name,
            body,
            [s["done"][0], state["step"], state["out"]],
            [((unit, sz.width), f32), ((unit, sz.width), f32), ((extra, LANES), f32)],
            outs=[VMEM, HBM, HBM],
            alias={2: 0},
            scratch=[pltpu.SemaphoreType.DMA((2,))],
        )

    for what in ORDER:
        if what == "V":
            start_vector()
        elif what[0] == "K":
            start(what[1], (int(what[2]),) if what[2:] else (1, 0))
        elif what[0] == "f":
            fold(what[1])
        elif what[1] == "1":
            first_sum(what[0])
        elif what[1] == "4":
            finish(what[0])
        elif what[1] == "5":
            (place_last if what[0] == LAST else place_blocks)(what[0])
        else:
            next_sum(what[0], int(what[1]) - 1)
    return state["out"], state["step"].reshape(-1)


def coupled(slices, slice_mix, lengths):
    count = slices.shape[0]
    coupling = (slice_mix + slice_mix.T) * 0.5 * (1.0 - jnp.eye(count, dtype=jnp.float32))
    blocks = lengths.shape[1]
    position = lax.broadcasted_iota(jnp.int32, (blocks, slices.shape[1] // blocks), 1)
    used = (position < lengths[0][:, None]).reshape(-1).astype(jnp.float32)
    out = []
    for k in range(count):
        total = coupling[k, 0] * slices[0].astype(jnp.float32)
        for l in range(1, count):
            total = total + coupling[k, l] * slices[l].astype(jnp.float32)
        out.append(total)
    return (jnp.stack(out) * used[None, :, None]).astype(jnp.bfloat16)


def whole(slices, slice_mix, lengths, search_step):
    width = slices.shape[2]
    left = slices.reshape(-1, width)
    right = coupled(slices, slice_mix, lengths).reshape(-1, width)
    rows = lax.psum_scatter(
        lax.dot_general(left, right, DIMS0, preferred_element_type=jnp.float32), AXIS, scatter_dimension=0, tiled=True
    )
    applied = jnp.dot(right, search_step, preferred_element_type=jnp.float32)
    head = applied.astype(jnp.bfloat16)
    tail = (applied - head.astype(jnp.float32)).astype(jnp.bfloat16)
    share = lax.dot_general(left, head, DIMS0, preferred_element_type=jnp.float32)
    share = share + lax.dot_general(left, tail, DIMS0, preferred_element_type=jnp.float32)
    return rows, lax.psum(share, AXIS)


def solution(mesh):
    devices = mesh.shape[AXIS]

    def on_device(slices, slice_mix, lengths, search_step):
        if fits(devices, slices, lengths):
            return halved(Sizes(devices, slices, lengths), slices, slice_mix, lengths, search_step)
        return whole(slices, slice_mix, lengths, search_step)

    return jax.shard_map(
        on_device,
        mesh=mesh,
        in_specs=(
            P(None, ("groups", AXIS), None),
            P(),
            P(("groups", AXIS), None),
            P("groups"),
        ),
        out_specs=(P(("groups", AXIS), None), P("groups")),
        check_vma=False,
    )
```
